32 devices in a mesh: clips: 2 (over x), rows: 16 (over z, y, core).
Axes of the slice: x: 2, y: 2, z: 4, core: 2. Of those that a mesh axis runs over, the one named last changes fastest.
Arguments:
- latents: bfloat16 [8, 64, 160, 384], P('clips', 'rows'), parts along dimension 0, may hold values from -6 to 6
- gamma: float32 [384], replicated, may hold values from 0.5 to 1.5
- weight: bfloat16 [3, 3, 3, 384, 384], replicated, may hold values from -0.0625 to 0.0625
- bias: float32 [384], replicated, may hold values from -3 to 3
- intersection: int32 [32], P('clips'), parts along dimension 0, may hold values from 0 to 2
- ramp: int32 [32], P('clips'), parts along dimension 0, may hold values from 1 to 3
Outputs:
- decoded: bfloat16 [8, 64, 160, 384], P('clips', 'rows'), parts along dimension 0
The draws below stay inside these ranges and needn't reach their ends.
There are 2 independent parts, one for each index of `clips`. The reference program is written for one: setup_inputs(seed, part) draws one part's arguments, and reference() takes and returns one part's arrays. A program takes and returns all parts, laid end to end along the dimension named above; an argument that names none is the same for every part. Nothing has to cross between parts.
All inputs are finite; a program needn't handle non-finite values.
Results may differ from the reference program's by a relative error of at most 0.0034.
Values may be sent and summed in bfloat16 or wider, within the bound.
No kernel may reach another device: no remote copies, remote signals or barrier semaphores. Data moves between devices by JAX's collectives and lax.ppermute only.
A program may use at most 448 MiB of HBM per device.

```python
import jax
import jax.numpy as jnp
from jax import lax

C = 384
W = 160
FRAMES = 4
ROWS_DEV = 4
OV_MAX = 2
TILES = 16
H = 64


def with_ends(values, stream_key, smallest, largest):
    shape = values.shape
    index_at = [jax.random.randint(jax.random.fold_in(stream_key, axis), (), 0, shape[axis]) for axis in range(len(shape))]
    values = values.at[tuple(index_at)].set(smallest)
    longest = shape.index(max(shape))
    index_at[longest] = (index_at[longest] + 1) % shape[longest]
    return values.at[tuple(index_at)].set(largest)


def block_scale(stream_key, shape, shards, low, largest):
    factor_of, own = 1.0, jax.random.fold_in(stream_key, 6)
    for position, parts in shards:
        heights = jnp.exp(jax.random.uniform(jax.random.fold_in(own, position), (parts,), jnp.float32, low / len(shards), largest / len(shards)))
        factor_of = factor_of * jnp.repeat(heights, shape[position] // parts).reshape([-1 if axis == position else 1 for axis in range(len(shape))])
    return factor_of


def scatter_about(rng, extent, scale, most, cuts=(), held_as=jnp.bfloat16):
    drawn = jax.random.normal(rng, extent, jnp.float32) * scale
    if len(cuts) > 0:
        drawn = block_scale(rng, extent, cuts, -0.22, 0.18) * drawn
    return jnp.clip(drawn, min=-most, max=most).astype(held_as)


def setup_inputs(seed: int = 0, part: int = 0) -> dict:
    splits = jax.random.split(jax.random.key(seed), 7)
    own_keys = jax.random.split(jax.random.fold_in(splits[6], part), 7)
    return {
        "latents": scatter_about(own_keys[0], (FRAMES, H, W, C), 1.0, 6.0, ((1, 16),)),
        "gamma": jnp.clip(jax.random.uniform(splits[1], (C,), jnp.float32, 0.5, 1.5), 0.5, 1.5),
        "weight": scatter_about(splits[2], (3, 3, 3, C, C), (27 * C) ** -0.5, 0.0625),
        "bias": scatter_about(splits[3], (C,), 0.5, 3.0, (), jnp.float32),
        "intersection": with_ends(jax.random.randint(own_keys[4], (TILES,), 0, OV_MAX + 1), jax.random.fold_in(own_keys[4], 1), 0, OV_MAX).astype(jnp.int32),
        "ramp": with_ends(jax.random.randint(own_keys[5], (TILES,), 1, 4), jax.random.fold_in(own_keys[5], 1), 1, 3).astype(jnp.int32),
    }


def activate(tile, gamma, keep):
    values = tile.astype(jnp.float32)
    square = lax.optimization_barrier(jnp.mean(values * values, axis=-1, keepdims=True))
    normed = values * lax.rsqrt(square + 1e-06) * gamma
    return (jax.nn.silu(normed) * keep).astype(jnp.bfloat16)

def convolve(stacked, weight, bias, count):
    padded = jnp.pad(stacked, ((0, 0), (1, 1), (1, 1), (0, 0)))
    height = stacked.shape[1]
    width = stacked.shape[2]
    total = jnp.zeros((count, height, width, weight.shape[4]), jnp.float32)
    for step_t in range(3):
        for step_h in range(3):
            for step_w in range(3):
                slab = padded[step_t:step_t + count, step_h:step_h + height, step_w:step_w + width]
                total = total + jnp.einsum('fhwc,cd->fhwd', slab, weight[step_t, step_h, step_w], preferred_element_type=jnp.float32)
    return total + bias

def decode_tile(tile, keep, gamma, weight, bias):
    act = activate(tile, gamma, keep)
    stacked = jnp.pad(act, ((2, 0), (0, 0), (0, 0), (0, 0)))
    return (tile.astype(jnp.float32) + convolve(stacked, weight, bias, tile.shape[0])).astype(jnp.bfloat16)

def reference(latents, gamma, weight, bias, intersection, ramp):
    rows = ROWS_DEV
    extra = OV_MAX
    tiles = TILES
    padded = jnp.pad(latents, ((0, 0), (0, extra), (0, 0), (0, 0)))
    numbers = jnp.arange(tiles, dtype=jnp.int32)
    eff = jnp.where(numbers == tiles - 1, 0, intersection).astype(jnp.int32)
    places = jnp.arange(rows + extra, dtype=jnp.int32)

    def one_tile(number):
        tile = lax.dynamic_slice_in_dim(padded, (number * rows).astype(jnp.int32), rows + extra, 1)
        keep = (places < rows + eff[number]).astype(jnp.float32).reshape(1, -1, 1, 1)
        return decode_tile(tile, keep, gamma, weight, bias)
    outs = lax.map(one_tile, numbers)
    own = outs[:, :, :rows]
    ext = outs[:, :, rows:]
    prev_ext = jnp.concatenate([jnp.zeros_like(ext[:1]), ext[:-1]], axis=0)
    prev_ov = jnp.concatenate([jnp.zeros((1,), jnp.int32), eff[:-1]], axis=0)
    prev_ramp = jnp.concatenate([jnp.zeros((1,), jnp.int32), ramp[:-1]], axis=0)
    offsets = jnp.arange(extra, dtype=jnp.int32)
    blend_w = jnp.where(offsets[None, :] < prev_ov[:, None], jnp.maximum(prev_ramp[:, None] - offsets[None, :], 0).astype(jnp.float32) / (prev_ramp[:, None] + 1).astype(jnp.float32), jnp.float32(0.0)).astype(jnp.float32)
    blend_w = blend_w.reshape(tiles, 1, extra, 1, 1)
    head = own[:, :, :extra].astype(jnp.float32)
    mixed = (blend_w * prev_ext.astype(jnp.float32) + (1.0 - blend_w) * head).astype(jnp.bfloat16)
    result = jnp.concatenate([mixed, own[:, :, extra:]], axis=2)
    result = jnp.transpose(result, (1, 0, 2, 3, 4))
    return result.reshape(result.shape[0], tiles * rows, result.shape[3], result.shape[4])
```

```python
import jax
import jax.numpy as jnp
from jax import lax
from jax.experimental import pallas as pl
from jax.experimental.pallas import tpu as pltpu
from jax.sharding import PartitionSpec as P

F32 = jnp.float32
BF16 = jnp.bfloat16
TAPS = 3


def shifted(block, axis, distance):
    devices = range(lax.axis_size(axis))
    route = [(i - distance, i) for i in devices if i - distance in devices]
    return lax.ppermute(block, axis, route)


def coefficients(inter_ref, ramp_ref, chans):
    index = lax.axis_index("rows")
    count = lax.axis_size("rows")
    previous = jnp.maximum(index - 1, 0)
    own = jnp.where(index == count - 1, 0, inter_ref[index])
    before = jnp.where(index > 0, inter_ref[previous], 0)
    row = lambda scalar: jnp.full((1, chans), scalar, jnp.int32)
    own, before, ramp = row(own), row(before), row(ramp_ref[previous])
    steps = (ramp + 1).astype(F32)
    first = jnp.where(before > 0, jnp.maximum(ramp, 0).astype(F32) / steps, 0.0)
    second = jnp.where(before > 1, jnp.maximum(ramp - 1, 0).astype(F32) / steps, 0.0)
    top = first
    below_first = jnp.where(before > 1, 1.0, 1.0 - first)
    below_second = 1.0 - second
    bottom = jnp.where(own > 0, 1.0, 0.0)
    return top, below_first, below_second, bottom


def activate(values, gamma):
    square = jnp.mean(values * values, axis=-1, keepdims=True)
    normed = values * lax.rsqrt(square + 1e-06) * gamma
    half = 0.5 * normed
    return half + half * jnp.tanh(half)


def spread(act, line, targets):
    width, chans = act.shape
    line[8 : 8 + width] = act
    for step in range(TAPS):
        piece = act if step == 1 else line[7 + step : 7 + step + width]
        for target, scale in targets:
            part = piece.astype(BF16)
            if scale is not None:
                part = (part.astype(F32) * scale).astype(BF16)
            target[:, step * chans : (step + 1) * chans] = part


def interior(
    inter_ref, ramp_ref, x_hbm, w_hbm, gamma_ref, bias_ref,
    out_hbm, part_hbm,
    x_s, w_s, line, flat, scaled, acc, done_s, part_s, x_sem, w_sem, o_sem, p_sem,
):
    frames, rows, width, chans = x_s.shape
    deep = TAPS * chans
    x_in = [pltpu.make_async_copy(x_hbm.at[f], x_s.at[f], x_sem.at[f]) for f in range(frames)]
    x_in[0].start()
    w_in = {}
    for slot in range(TAPS):
        for kh in range(TAPS):
            w_in[slot, kh] = pltpu.make_async_copy(
                w_hbm.at[TAPS - 1 - slot, kh],
                w_s.at[pl.ds(kh * deep, deep), pl.ds(slot * chans, chans)],
                w_sem.at[slot, kh],
            )
    for kh in range(TAPS):
        w_in[0, kh].start()
    for f in range(1, frames):
        x_in[f].start()
    for slot in range(1, TAPS):
        for kh in range(TAPS):
            w_in[slot, kh].start()
    _, below_first, below_second, _ = coefficients(inter_ref, ramp_ref, chans)
    gamma = gamma_ref[...]
    bias = bias_ref[...]
    line[:, 0:8] = jnp.zeros((rows, 8, chans), F32)
    line[:, 8 + width : 16 + width] = jnp.zeros((rows, 8, chans), F32)

    def prepare(f):
        x_in[f].wait()
        for h in range(rows):
            act = activate(x_s[f, h].astype(F32), gamma)
            targets = [(flat.at[f, h], None)]
            if h == 1:
                targets.append((scaled.at[f, 0], below_first))
            if h == 2:
                targets.append((scaled.at[f, 1], below_second))
            spread(act, line.at[h], targets)

    copies = []
    for f in range(frames):
        prepare(f)
        if f == 0:
            for copy in w_in.values():
                copy.wait()
        wide = min(TAPS, frames - f) * chans
        weight = lambda low, high: w_s[low * deep : high * deep, :wide]
        for r in range(rows):
            if r == 0:
                left = jnp.concatenate([flat[f, 0], scaled[f, 0]], axis=1)
                right = weight(1, 3)
            elif r == rows - 1:
                left = jnp.concatenate([flat[f, r - 1], flat[f, r]], axis=1)
                right = weight(0, 2)
            else:
                last = scaled[f, 1] if r == 1 else flat[f, r + 1]
                left = jnp.concatenate([flat[f, r - 1], flat[f, r], last], axis=1)
                right = weight(0, 3)
            product = jnp.dot(left, right, preferred_element_type=F32)
            for slot in range(min(TAPS, frames - f)):
                g = f + slot
                term = product[:, slot * chans : (slot + 1) * chans]
                if f == 0 or slot == 2:
                    acc[g, r] = term
                else:
                    acc[g, r] += term
        for r in range(rows):
            total = acc[f, r] + (x_s[f, r].astype(F32) + bias)
            if r == 0:
                part_s[f, 0] = total
            elif r == rows - 1:
                part_s[f, 1] = total
            else:
                done_s[f, r - 1] = total.astype(BF16)
        copies.append(pltpu.make_async_copy(
            done_s.at[f], out_hbm.at[f, pl.ds(1, rows - 2)], o_sem.at[f]))
        copies[-1].start()
        copies.append(pltpu.make_async_copy(part_s.at[f], part_hbm.at[f], p_sem.at[f]))
        copies[-1].start()
    for copy in copies:
        copy.wait()


def edges(
    inter_ref, ramp_ref, top_hbm, bottom_hbm, w_hbm, gamma_ref, part_hbm, _,
    out_hbm,
    h_s, w_s, line, flat, acc, part_s, done_s, h_sem, w_sem, p_sem, o_sem,
):
    _, frames, width, chans = h_s.shape
    deep = TAPS * chans
    rows = out_hbm.shape[1]
    h_in = [
        pltpu.make_async_copy(source, h_s.at[side], h_sem.at[side])
        for side, source in enumerate((top_hbm, bottom_hbm))
    ]
    for copy in h_in:
        copy.start()
    w_in = []
    for side in range(2):
        for slot in range(TAPS):
            w_in.append(pltpu.make_async_copy(
                w_hbm.at[TAPS - 1 - slot, 2 * side],
                w_s.at[side, :, pl.ds(slot * chans, chans)],
                w_sem.at[side, slot],
            ))
            w_in[-1].start()
    p_in = pltpu.make_async_copy(part_hbm, part_s, p_sem)
    p_in.start()
    top, _, _, bottom = coefficients(inter_ref, ramp_ref, chans)
    gamma = gamma_ref[...]
    line[:, 0:8] = jnp.zeros((2, 8, chans), F32)
    line[:, 8 + width : 16 + width] = jnp.zeros((2, 8, chans), F32)
    for copy in h_in:
        copy.wait()
    for f in range(frames):
        for side, scale in enumerate((top, bottom)):
            act = activate(h_s[side, f].astype(F32), gamma)
            spread(act, line.at[side], [(flat.at[side, f], scale)])
    for copy in w_in:
        copy.wait()
    p_in.wait()
    copies = []
    for side in range(2):
        for f in range(frames):
            count = min(TAPS, frames - f)
            product = jnp.dot(
                flat[side, f], w_s[side, :, : count * chans], preferred_element_type=F32
            )
            for slot in range(count):
                part_s[f + slot, side] += product[:, slot * chans : (slot + 1) * chans]
            done_s[f, side] = part_s[f, side].astype(BF16)
            copies.append(pltpu.make_async_copy(
                done_s.at[f, side], out_hbm.at[f, side * (rows - 1)], o_sem.at[f, side]))
            copies[-1].start()
    for copy in copies:
        copy.wait()


def per_device(latents, gamma, weight, bias, intersection, ramp):
    frames, rows, width, chans = latents.shape
    deep = TAPS * chans
    gamma = gamma.reshape(1, chans)
    bias = bias.reshape(1, chans)
    weight = weight.reshape(TAPS, TAPS, deep, chans)
    top = shifted(latents[:, rows - 1], "rows", 1)
    bottom = shifted(latents[:, 0], "rows", -1)
    smem = pl.BlockSpec(memory_space=pltpu.SMEM)
    vmem = pl.BlockSpec(memory_space=pltpu.VMEM)
    hbm = pl.BlockSpec(memory_space=pl.ANY)
    dma = pltpu.SemaphoreType.DMA
    out, part = pl.pallas_call(
        interior,
        out_shape=(
            jax.ShapeDtypeStruct(latents.shape, BF16),
            jax.ShapeDtypeStruct((frames, 2, width, chans), F32),
        ),
        in_specs=[smem, smem, hbm, hbm, vmem, vmem],
        out_specs=(hbm, hbm),
        scratch_shapes=[
            pltpu.VMEM((frames, rows, width, chans), BF16),
            pltpu.VMEM((TAPS * deep, TAPS * chans), BF16),
            pltpu.VMEM((rows, width + 16, chans), F32),
            pltpu.VMEM((frames, rows, width, deep), BF16),
            pltpu.VMEM((frames, 2, width, deep), BF16),
            pltpu.VMEM((frames, rows, width, chans), F32),
            pltpu.VMEM((frames, rows - 2, width, chans), BF16),
            pltpu.VMEM((frames, 2, width, chans), F32),
            dma((frames,)),
            dma((TAPS, TAPS)),
            dma((frames,)),
            dma((frames,)),
        ],
        cost_estimate=pl.CostEstimate(
            flops=2 * 90 * width * deep * chans, bytes_accessed=14 * 2**20, transcendentals=0
        ),
        compiler_params=pltpu.CompilerParams(vmem_limit_bytes=50 * 2**20),
        name="interior",
    )(intersection, ramp, latents, weight, gamma, bias)
    return pl.pallas_call(
        edges,
        out_shape=jax.ShapeDtypeStruct(latents.shape, BF16),
        in_specs=[smem, smem, hbm, hbm, hbm, vmem, hbm, hbm],
        out_specs=hbm,
        input_output_aliases={7: 0},
        scratch_shapes=[
            pltpu.VMEM((2, frames, width, chans), BF16),
            pltpu.VMEM((2, deep, TAPS * chans), BF16),
            pltpu.VMEM((2, width + 16, chans), F32),
            pltpu.VMEM((2, frames, width, deep), BF16),
            pltpu.VMEM((8, 128), F32),
            pltpu.VMEM((frames, 2, width, chans), F32),
            pltpu.VMEM((frames, 2, width, chans), BF16),
            dma((2,)),
            dma((2, TAPS)),
            dma(()),
            dma((frames, 2)),
        ],
        cost_estimate=pl.CostEstimate(
            flops=2 * 18 * width * deep * chans, bytes_accessed=9 * 2**20, transcendentals=0
        ),
        compiler_params=pltpu.CompilerParams(vmem_limit_bytes=40 * 2**20),
        name="edges",
    )(intersection, ramp, top, bottom, weight, gamma, part, out)


def solution(mesh):
    in_specs = (P("clips", "rows", None, None), P(), P(), P(), P("clips"), P("clips"))
    out_specs = P("clips", "rows", None, None)
    return jax.shard_map(
        per_device, mesh=mesh, in_specs=in_specs, out_specs=out_specs, check_vma=False
    )
```

```python
import jax
import jax.numpy as jnp
from jax import lax
from jax.experimental import pallas as pl
from jax.experimental.pallas import tpu as pltpu
from jax.sharding import PartitionSpec as P

F32 = jnp.float32
BF16 = jnp.bfloat16
TAPS = 3
LANES = 128
SIDE = 256
CHUNK = 32
MXUS = 2
ACCS = 6


def scales(inter_ref, ramp_ref):
    index = lax.axis_index("rows")
    count = lax.axis_size("rows")
    previous = jnp.maximum(index - 1, 0)
    own = jnp.where(index == count - 1, 0, inter_ref[index])
    before = jnp.where(index > 0, inter_ref[previous], 0)
    row = lambda scalar: jnp.full((1, LANES), scalar, jnp.int32)
    own, before, ramp = row(own), row(before), row(ramp_ref[previous])
    steps = (ramp + 1).astype(F32)
    first = jnp.where(before > 0, jnp.maximum(ramp, 0).astype(F32) / steps, 0.0)
    second = jnp.where(before > 1, jnp.maximum(ramp - 1, 0).astype(F32) / steps, 0.0)
    below_first = jnp.where(before > 1, 1.0, 1.0 - first)
    bottom = jnp.where(own > 0, 1.0, 0.0)
    return first, below_first, 1.0 - second, bottom


def parity():
    return lax.rem(lax.axis_index("rows"), 2)


def activate(values, gamma):
    square = jnp.mean(values * values, axis=-1, keepdims=True)
    normed = values * lax.rsqrt(square + 1e-06) * gamma
    half = 0.5 * normed
    return half + half * jnp.tanh(half)


def prepare(source, gamma, line, target):
    width, chans = source.shape

    def first(at):
        act = activate(source[at : at + CHUNK].astype(F32), gamma)
        line[8 + at : 8 + at + CHUNK] = act
        target[at : at + CHUNK, chans : 2 * chans] = act.astype(BF16)

    def second(at):
        for step in (0, 2):
            piece = line[7 + step + at : 7 + step + at + CHUNK]
            target[at : at + CHUNK, step * chans : (step + 1) * chans] = piece.astype(BF16)

    for at in range(0, width, CHUNK):
        yield lambda at=at: first(at)
    for at in range(0, width, CHUNK):
        yield lambda at=at: second(at)


def clear_ends(line):
    lines, padded, chans = line.shape
    line[:, 0:8] = jnp.zeros((lines, 8, chans), F32)
    line[:, padded - 8 : padded] = jnp.zeros((lines, 8, chans), F32)


class Queue:
    def __init__(self):
        self.items = []
        self.done = 0

    def add(self, steps):
        self.items.extend(steps)
        return len(self.items)

    def until(self, mark):
        while self.done < mark:
            self.items[self.done]()
            self.done += 1

    def some(self, number):
        self.until(min(len(self.items), self.done + number))


def tiles_of(chans, count):
    blocks = [(slot, block) for slot in range(count) for block in range(chans // LANES)]
    return [blocks[i : i + 2] for i in range(0, len(blocks), 2)]


def jobs_of(tiles, rows):
    full = range(rows)
    jobs = [
        [(tiles[i], full), (tiles[i + 1], full)] for i in range(0, len(tiles) - 1, 2)
    ]
    if len(tiles) % 2:
        jobs.append([(tiles[-1], full[: rows // 2]), (tiles[-1], full[rows // 2 :])])
    return jobs


def in_pairs(chunks):
    return [chunks[i : i + 2] for i in range(0, len(chunks), 2)]


def cells(w_ref, tile, places):
    columns = []
    for slot, block in tile:
        parts = [
            w_ref[TAPS - 1 - slot, kh, rest * LANES : (rest + 1) * LANES,
                  block * LANES : (block + 1) * LANES]
            for kh, rest in places
        ]
        while len(parts) < 2:
            parts.append(jnp.zeros((LANES, LANES), BF16))
        columns.append(jnp.concatenate(parts, axis=0))
    while len(columns) < 2:
        columns.append(jnp.zeros((SIDE, LANES), BF16))
    return jnp.concatenate(columns, axis=1)


def beside(parts):
    while len(parts) < 2:
        parts = parts + [jnp.zeros_like(parts[0])]
    return jnp.concatenate(parts, axis=1)


class Units:
    def __init__(self, accs):
        self.accs = [accs[m * ACCS : (m + 1) * ACCS] for m in range(MXUS)]
        self.stage = [0] * MXUS
        self.load = [None] * MXUS

    def weights(self, m, operand):
        pltpu.matmul_push_rhs(operand, self.stage[m], m)
        self.load[m] = self.stage[m]
        self.stage[m] = 1 - self.stage[m]

    def add(self, m, number, block):
        pltpu.matmul_acc_lhs(self.accs[m][number], block, self.load[m])
        self.load[m] = None

    def pop(self, m, number):
        return pltpu.matmul_pop(self.accs[m][number])


def conv_passes(depth):
    return in_pairs([divmod(chunk, depth) for chunk in range(TAPS * depth)])


def acc_of(r, places, rows):
    if not any(0 <= r + kh - 1 < rows for kh, _ in places):
        return None
    if r < 2 and places[-1][0] == 2:
        return 4 + r
    return r


def row_block(flat_row, r, places):
    parts = []
    for kh, rest in places:
        h = r + kh - 1
        if h < 0:
            parts.append(jnp.zeros((flat_row(0).shape[0], LANES), BF16))
        else:
            parts.append(flat_row(h)[:, rest * LANES : (rest + 1) * LANES])
    return beside(parts)


def matrix_job(units, job, passes, rows, flat_row, weight, step, pop, between=None):
    for number, places in enumerate(passes):
        active = [
            (m, tile, [r for r in rows_of if acc_of(r, places, rows) is not None])
            for m, (tile, rows_of) in enumerate(job)
        ]
        for m, tile, rows_of in active:
            if rows_of:
                units.weights(m, weight(tile, places))
        for r in (3, 1, 2, 0):
            if any(r in rows_of for _, _, rows_of in active):
                block = row_block(flat_row, r, places)
                for m, _, rows_of in active:
                    if r in rows_of:
                        units.add(m, acc_of(r, places, rows), block)
        if between is not None and number == len(passes) - 3:
            between()
        for r in (3, 1, 0, 2):
            here = acc_of(r, places, rows)
            later = [acc_of(r, other, rows) for other in passes[number + 1 :]]
            if here is not None and here not in later:
                last = all(other is None for other in later)
                for m, (tile, rows_of) in enumerate(job):
                    if r in rows_of:
                        pop(m, tile, here, r, last)
        step()


def select(x_hbm, far_ref, near_ref, sem):
    frames, rows = x_hbm.shape[:2]
    odd = parity()
    copies = []
    for place, (target, row) in enumerate(
        ((far_ref, odd * (rows - 1)), (near_ref, (1 - odd) * (rows - 1)))
    ):
        copies.append(pltpu.make_async_copy(x_hbm.at[:, row], target, sem.at[place]))
        copies[-1].start()
    for copy in copies:
        copy.wait()


def interior(
    inter_ref, ramp_ref, x_ref, near_ref, w_hbm, gamma_ref, bias_ref,
    out_hbm, part_ref, w_ref, last_ref, carry_ref, nacc_ref,
    line, flat, nflat, acc, done_s, w_sem, o_sem,
):
    frames, rows, width, chans = x_ref.shape
    depth = TAPS * chans // LANES
    passes = conv_passes(depth)
    order = [(slot, kh) for slots in ((0, 1), (2,)) for kh in range(TAPS) for slot in slots]
    w_in = {
        (slot, kh): pltpu.make_async_copy(
            w_hbm.at[TAPS - 1 - slot, kh], w_ref.at[TAPS - 1 - slot, kh], w_sem.at[slot, kh])
        for slot, kh in order
    }
    starts = [w_in[key].start for key in order]
    for start in starts[:4]:
        start()
    starts = starts[4:]
    _, below_first, below_second, _ = scales(inter_ref, ramp_ref)
    below = (below_first, below_second)
    gamma = gamma_ref[...]
    clear_ends(line)
    near_kh = 2 * (1 - parity())

    def flat_at(f, h):
        return last_ref.at[h] if f == frames - 1 else flat.at[f, h]

    queue = Queue()
    ready = {}
    for f in range(frames):
        for h in reversed(range(rows)):
            ready[f, h] = queue.add(
                prepare(x_ref.at[f, h], gamma, line.at[h], flat_at(f, h)))
        ready[f] = queue.add(prepare(near_ref.at[f], gamma, line.at[rows], nflat.at[f]))

    def weight(tile, places):
        for slot, _ in tile:
            for kh, _ in places:
                copy = w_in.pop((slot, kh), None)
                if copy is not None:
                    copy.wait()
        return cells(w_ref, tile, places)

    def contribute(g, r, lanes, term, first, final):
        if first:
            term = term + (x_ref[g, r, :, lanes].astype(F32) + bias_ref[:, lanes])
        else:
            term = term + acc[g, r, :, lanes]
        if not final:
            acc[g, r, :, lanes] = term
        elif r == 0:
            part_ref[g, 0, :, lanes] = term
        elif r == rows - 1:
            part_ref[g, 1, :, lanes] = term
        else:
            done_s[g, r - 1, :, lanes] = term.astype(BF16)

    def run(*accs):
        units = Units(accs)

        def pop(f, m, tile, number, r, last):
            product = units.pop(m, number)
            for i, (slot, block) in enumerate(tile):
                lanes = slice(block * LANES, (block + 1) * LANES)
                term = product[:, i * LANES : (i + 1) * LANES]
                if number >= 4:
                    term = term * below[r]
                contribute(
                    f + slot, r, lanes, term,
                    (f == 0 or slot == 2) and number < 4, slot == 0 and last)

        def near(f, job):
            queue.until(ready[f])
            for places in in_pairs([(near_kh, c) for c in range(depth)]):
                low, high = places[0][1] * LANES, (places[-1][1] + 1) * LANES
                for m, (tile, _) in enumerate(job):
                    if m == 0 or tile is not job[0][0]:
                        units.weights(m, cells(w_ref, tile, places))
                        block = nflat[f, :, low:high]
                        units.add(m, 0, block if len(places) == 2 else beside([block]))

        def near_pop(f, job):
            for m, (tile, _) in enumerate(job):
                if m == 0 or tile is not job[0][0]:
                    product = units.pop(m, 0)
                    for i, (slot, block) in enumerate(tile):
                        lanes = slice(block * LANES, (block + 1) * LANES)
                        term = product[:, i * LANES : (i + 1) * LANES]
                        if f > 0 and slot < 2:
                            term = term + nacc_ref[f + slot, :, lanes]
                        nacc_ref[f + slot, :, lanes] = term

        queue.until(ready[0, 3] if rows == 4 else ready[0, 0])
        for start in starts[:3]:
            start()
        queue.until(ready[0, 2] if rows == 4 else ready[0, 0])
        for start in starts[3:]:
            start()
        for f in range(frames - 1):
            jobs = jobs_of(tiles_of(chans, min(TAPS, frames - f)), rows)
            for place, job in enumerate(jobs):
                flat_row = lambda h: flat.at[f, h]
                if f == 0 and place == 0:
                    for r in reversed(range(rows)):
                        queue.until(ready[0, max(r - 1, 0)])
                        matrix_job(
                            units, [(tile, [r]) for tile, _ in job], passes, rows, flat_row,
                            weight, lambda: queue.some(1),
                            lambda *rest: pop(f, *rest))
                    near(f, job)
                    near_pop(f, job)
                else:
                    queue.until(ready[f])
                    matrix_job(
                        units, job, passes, rows, flat_row, weight,
                        lambda: queue.some(2), lambda *rest: pop(f, *rest),
                        lambda: near(f, job))
                    near_pop(f, job)
            copy = pltpu.make_async_copy(
                done_s.at[f], out_hbm.at[f, pl.ds(1, rows - 2)], o_sem.at[f])
            copy.start()
        f = frames - 1
        queue.until(ready[f])
        tiles = tiles_of(chans, 1)
        job = [(tile, None) for tile in tiles]
        near(f, job)
        near_pop(f, job)
        for r in range(rows):
            carry_ref[r] = acc[f, r]
        for f in range(frames - 1):
            pltpu.make_async_copy(
                done_s.at[f], out_hbm.at[f, pl.ds(1, rows - 2)], o_sem.at[f]).wait()

    pl.run_scoped(run, *[pltpu.ACC(m)((width, SIDE), F32) for m in range(MXUS) for _ in range(ACCS)])


def edges(
    inter_ref, ramp_ref, far_ref, w_ref, gamma_ref, part_ref, last_ref, carry_ref, nacc_ref, _,
    out_hbm,
    line, fflat, acc, facc, tail, done_s, inner_s, o_sem, i_sem,
):
    frames, width, chans = far_ref.shape
    rows = out_hbm.shape[1]
    depth = TAPS * chans // LANES
    passes = conv_passes(depth)
    odd = parity()
    top, below_first, below_second, bottom = scales(inter_ref, ramp_ref)
    below = (below_first, below_second)
    far_scale = jnp.where(odd == 1, bottom, top)
    near_scale = jnp.where(odd == 1, top, bottom)
    gamma = gamma_ref[...]
    clear_ends(line)
    final = frames - 1
    blocks = [slice(b * LANES, (b + 1) * LANES) for b in range(chans // LANES)]

    queue = Queue()
    ready = [
        queue.add(prepare(far_ref.at[f], gamma, line.at[0], fflat.at[f])) for f in range(frames)
    ]

    def near_row(g, at):
        span = slice(at, at + CHUNK)
        for lanes in blocks:
            base = tail[1 - odd, span, lanes] if g == final else part_ref[g, 1 - odd, span, lanes]
            total = base + near_scale * nacc_ref[g, span, lanes]
            done_s[g, 1 - odd, span, lanes] = total.astype(BF16)

    def run(*accs):
        units = Units(accs)

        def pop(m, tile, number, r, last):
            product = units.pop(m, number)
            for i, (_, block) in enumerate(tile):
                lanes = blocks[block]
                term = product[:, i * LANES : (i + 1) * LANES]
                if number >= 4:
                    term = acc[r, :, lanes] + term * below[r]
                else:
                    term = carry_ref[r, :, lanes] + term
                if not last:
                    acc[r, :, lanes] = term
                elif r == 0 or r == rows - 1:
                    tail[0 if r == 0 else 1, :, lanes] = term
                else:
                    inner_s[r - 1, :, lanes] = term.astype(BF16)

        tiles = tiles_of(chans, 1)
        job = [(tile, range(rows)) for tile in tiles]
        matrix_job(
            units, job, passes, rows, lambda h: last_ref.at[h],
            lambda tile, places: cells(w_ref, tile, places), lambda: queue.some(2), pop)
        inner = pltpu.make_async_copy(
            inner_s, out_hbm.at[final, pl.ds(1, rows - 2)], i_sem)
        inner.start()
        for g in range(frames):
            queue.add([lambda g=g, at=at: near_row(g, at) for at in range(0, width, CHUNK)])
        whole = [
            (f, tile) for f in range(frames) for tile in tiles_of(chans, min(TAPS, frames - f))
        ]
        for number, pair in enumerate(in_pairs(whole)):
            queue.until(ready[max(f for f, _ in pair)])
            here = (number % 2) * 3
            for places in in_pairs([(2 * odd, c) for c in range(depth)]):
                low, high = places[0][1] * LANES, (places[-1][1] + 1) * LANES
                for m, (f, tile) in enumerate(pair):
                    units.weights(m, cells(w_ref, tile, places))
                for m, (f, tile) in enumerate(pair):
                    block = fflat[f, :, low:high]
                    units.add(m, here, block if len(places) == 2 else beside([block]))
                queue.some(1)
            for m, (f, tile) in enumerate(pair):
                product = units.pop(m, here)
                for i, (slot, block) in enumerate(tile):
                    g = f + slot
                    lanes = blocks[block]
                    term = product[:, i * LANES : (i + 1) * LANES]
                    if f > 0 and slot < 2:
                        term = term + facc[g, :, lanes]
                    if slot > 0:
                        facc[g, :, lanes] = term
                        continue
                    base = tail[odd, :, lanes] if g == final else part_ref[g, odd, :, lanes]
                    done_s[g, odd, :, lanes] = (base + far_scale * term).astype(BF16)
        queue.until(len(queue.items))
        copies = []
        for f in range(frames):
            for side in range(2):
                copies.append(pltpu.make_async_copy(
                    done_s.at[f, side], out_hbm.at[f, side * (rows - 1)], o_sem.at[f, side]))
                copies[-1].start()
        inner.wait()
        for copy in copies:
            copy.wait()

    pl.run_scoped(run, *[pltpu.ACC(m)((width, SIDE), F32) for m in range(MXUS) for _ in range(ACCS)])


def per_device(latents, gamma, weight, bias, intersection, ramp):
    frames, rows, width, chans = latents.shape
    deep = TAPS * chans
    gamma = gamma.reshape(1, chans)
    bias = bias.reshape(1, chans)
    weight = weight.reshape(TAPS, TAPS, deep, chans)
    count = lax.axis_size("rows")
    smem = pl.BlockSpec(memory_space=pltpu.SMEM)
    vmem = pl.BlockSpec(memory_space=pltpu.VMEM)
    hbm = pl.BlockSpec(memory_space=pltpu.HBM)
    anywhere = pl.BlockSpec(memory_space=pl.ANY)
    dma = pltpu.SemaphoreType.DMA
    inside = lambda array: pltpu.with_memory_space_constraint(array, pltpu.VMEM)
    outside = lambda array: pltpu.with_memory_space_constraint(array, pltpu.HBM)
    swap = lambda array, start: lax.ppermute(array, "rows", [
        pair for k in range(start, count - 1, 2) for pair in ((k, k + 1), (k + 1, k))])
    halo = pltpu.VMEM((frames, width, chans), BF16)
    far, near = pl.pallas_call(
        select,
        out_shape=(halo, halo),
        in_specs=[hbm],
        out_specs=(vmem, vmem),
        scratch_shapes=[dma((2,))],
        name="select",
    )(outside(latents))
    near = swap(near, 0)
    far = swap(far, 1)
    out, part, weight, last, carry, nacc = pl.pallas_call(
        interior,
        out_shape=(
            jax.ShapeDtypeStruct(latents.shape, BF16),
            pltpu.VMEM((frames - 1, 2, width, chans), F32),
            pltpu.VMEM(weight.shape, BF16),
            pltpu.VMEM((rows, width, deep), BF16),
            pltpu.VMEM((rows, width, chans), F32),
            pltpu.VMEM((frames, width, chans), F32),
        ),
        in_specs=[smem, smem, vmem, vmem, hbm, vmem, vmem],
        out_specs=(anywhere,) + (vmem,) * 5,
        scratch_shapes=[
            pltpu.VMEM((rows + 1, width + 16, chans), F32),
            pltpu.VMEM((frames - 1, rows, width, deep), BF16),
            pltpu.VMEM((frames, width, deep), BF16),
            pltpu.VMEM((frames, rows, width, chans), F32),
            pltpu.VMEM((frames - 1, rows - 2, width, chans), BF16),
            dma((TAPS, TAPS)),
            dma((frames - 1,)),
        ],
        cost_estimate=pl.CostEstimate(
            flops=2 * 84 * width * deep * chans, bytes_accessed=14 * 2**20, transcendentals=0
        ),
        compiler_params=pltpu.CompilerParams(vmem_limit_bytes=24 * 2**20),
        name="interior",
    )(intersection, ramp, inside(latents), inside(near), outside(weight), gamma, bias)
    return pl.pallas_call(
        edges,
        out_shape=jax.ShapeDtypeStruct(latents.shape, BF16),
        in_specs=[smem, smem] + [vmem] * 7 + [anywhere],
        out_specs=anywhere,
        input_output_aliases={9: 0},
        scratch_shapes=[
            pltpu.VMEM((1, width + 16, chans), F32),
            pltpu.VMEM((frames, width, deep), BF16),
            pltpu.VMEM((rows, width, chans), F32),
            pltpu.VMEM((frames, width, chans), F32),
            pltpu.VMEM((2, width, chans), F32),
            pltpu.VMEM((frames, 2, width, chans), BF16),
            pltpu.VMEM((rows - 2, width, chans), BF16),
            dma((frames, 2)),
            dma(()),
        ],
        cost_estimate=pl.CostEstimate(
            flops=2 * 24 * width * deep * chans, bytes_accessed=4 * 2**20, transcendentals=0
        ),
        compiler_params=pltpu.CompilerParams(vmem_limit_bytes=16 * 2**20),
        name="edges",
    )(
        intersection, ramp, inside(far), inside(weight), gamma, inside(part), inside(last),
        inside(carry), inside(nacc), out,
    )


def solution(mesh):
    in_specs = (P("clips", "rows", None, None), P(), P(), P(), P("clips"), P("clips"))
    out_specs = P("clips", "rows", None, None)
    return jax.shard_map(
        per_device, mesh=mesh, in_specs=in_specs, out_specs=out_specs, check_vma=False
    )
```

```python
import jax
import jax.numpy as jnp
from jax import lax
from jax.experimental import pallas as pl
from jax.experimental.pallas import tpu as pltpu
from jax.sharding import PartitionSpec as P

F32 = jnp.float32
BF16 = jnp.bfloat16
TAPS = 3
LANES = 128
SIDE = 256
CHUNK = 32
MXUS = 2
ACCS = 6


def scales(inter_ref, ramp_ref):
    index = lax.axis_index("rows")
    count = lax.axis_size("rows")
    previous = jnp.maximum(index - 1, 0)
    own = jnp.where(index == count - 1, 0, inter_ref[index])
    before = jnp.where(index > 0, inter_ref[previous], 0)
    row = lambda scalar: jnp.full((1, LANES), scalar, jnp.int32)
    own, before, ramp = row(own), row(before), row(ramp_ref[previous])
    steps = (ramp + 1).astype(F32)
    first = jnp.where(before > 0, jnp.maximum(ramp, 0).astype(F32) / steps, 0.0)
    second = jnp.where(before > 1, jnp.maximum(ramp - 1, 0).astype(F32) / steps, 0.0)
    below_first = jnp.where(before > 1, 1.0, 1.0 - first)
    bottom = jnp.where(own > 0, 1.0, 0.0)
    return first, below_first, 1.0 - second, bottom


def parity():
    return lax.rem(lax.axis_index("rows"), 2)


def activate(values, half_gamma):
    square = jnp.mean(values * values, axis=-1, keepdims=True)
    half = values * lax.rsqrt(square + 1e-06) * half_gamma
    return half + half * jnp.tanh(half)


def prepare(source, gamma, line, target):
    width, chans = source.shape

    def first(at):
        act = activate(source[at : at + CHUNK].astype(F32), gamma)
        line[8 + at : 8 + at + CHUNK] = act
        target[at : at + CHUNK, chans : 2 * chans] = act.astype(BF16)

    def second(at):
        for step in (0, 2):
            piece = line[7 + step + at : 7 + step + at + CHUNK]
            target[at : at + CHUNK, step * chans : (step + 1) * chans] = piece.astype(BF16)

    for at in range(0, width, CHUNK):
        yield lambda at=at: first(at)
    for at in range(0, width, CHUNK):
        yield lambda at=at: second(at)


def clear_ends(line):
    lines, padded, chans = line.shape
    line[:, 0:8] = jnp.zeros((lines, 8, chans), F32)
    line[:, padded - 8 : padded] = jnp.zeros((lines, 8, chans), F32)


class Queue:
    def __init__(self):
        self.items = []
        self.done = 0

    def add(self, steps):
        self.items.extend(steps)
        return len(self.items)

    def until(self, mark):
        while self.done < mark:
            self.items[self.done]()
            self.done += 1

    def some(self, number):
        self.until(min(len(self.items), self.done + number))


def tiles_of(chans, count):
    blocks = [(slot, block) for slot in range(count) for block in range(chans // LANES)]
    return [blocks[i : i + 2] for i in range(0, len(blocks), 2)]


def jobs_of(tiles, rows):
    full = range(rows)
    jobs = [
        [(tiles[i], full), (tiles[i + 1], full)] for i in range(0, len(tiles) - 1, 2)
    ]
    if len(tiles) % 2:
        jobs.append([(tiles[-1], full[: rows // 2]), (tiles[-1], full[rows // 2 :])])
    return jobs


def in_pairs(chunks):
    return [chunks[i : i + 2] for i in range(0, len(chunks), 2)]


def cells(w_ref, tile, places):
    columns = []
    for slot, block in tile:
        parts = [
            w_ref[TAPS - 1 - slot, kh, rest * LANES : (rest + 1) * LANES,
                  block * LANES : (block + 1) * LANES]
            for kh, rest in places
        ]
        while len(parts) < 2:
            parts.append(jnp.zeros((LANES, LANES), BF16))
        columns.append(jnp.concatenate(parts, axis=0))
    while len(columns) < 2:
        columns.append(jnp.zeros((SIDE, LANES), BF16))
    return jnp.concatenate(columns, axis=1)


def beside(parts):
    while len(parts) < 2:
        parts = parts + [jnp.zeros_like(parts[0])]
    return jnp.concatenate(parts, axis=1)


class Units:
    def __init__(self, accs):
        self.accs = [accs[m * ACCS : (m + 1) * ACCS] for m in range(MXUS)]
        self.stage = [0] * MXUS
        self.load = [None] * MXUS

    def weights(self, m, operand):
        pltpu.matmul_push_rhs(operand, self.stage[m], m)
        self.load[m] = self.stage[m]
        self.stage[m] = 1 - self.stage[m]

    def add(self, m, number, block):
        pltpu.matmul_acc_lhs(self.accs[m][number], block, self.load[m])
        self.load[m] = None

    def pop(self, m, number):
        return pltpu.matmul_pop(self.accs[m][number])


def conv_passes(depth):
    return in_pairs([divmod(chunk, depth) for chunk in range(TAPS * depth)])


def acc_of(r, places, rows):
    if not any(0 <= r + kh - 1 < rows for kh, _ in places):
        return None
    if r < 2 and places[-1][0] == 2:
        return 4 + r
    return r


def row_block(flat_row, r, places):
    parts = []
    for kh, rest in places:
        h = r + kh - 1
        if h < 0:
            parts.append(jnp.zeros((flat_row(0).shape[0], LANES), BF16))
        else:
            parts.append(flat_row(h)[:, rest * LANES : (rest + 1) * LANES])
    return beside(parts)


def matrix_job(units, job, passes, rows, flat_row, weight, step, pop, between=None):
    for number, places in enumerate(passes):
        active = [
            (m, tile, [r for r in rows_of if acc_of(r, places, rows) is not None])
            for m, (tile, rows_of) in enumerate(job)
        ]
        for m, tile, rows_of in active:
            if rows_of:
                units.weights(m, weight(tile, places))
        for r in (3, 1, 2, 0):
            if any(r in rows_of for _, _, rows_of in active):
                block = row_block(flat_row, r, places)
                for m, _, rows_of in active:
                    if r in rows_of:
                        units.add(m, acc_of(r, places, rows), block)
        if between is not None and number == len(passes) - 3:
            between()
        for r in (3, 1, 0, 2):
            here = acc_of(r, places, rows)
            later = [acc_of(r, other, rows) for other in passes[number + 1 :]]
            if here is not None and here not in later:
                last = all(other is None for other in later)
                for m, (tile, rows_of) in enumerate(job):
                    if r in rows_of:
                        pop(m, tile, here, r, last)
        step()


def select(x_hbm, far_ref, near_ref, sem):
    frames, rows = x_hbm.shape[:2]
    odd = parity()
    copies = []
    for place, (target, row) in enumerate(
        ((far_ref, odd * (rows - 1)), (near_ref, (1 - odd) * (rows - 1)))
    ):
        copies.append(pltpu.make_async_copy(x_hbm.at[:, row], target, sem.at[place]))
        copies[-1].start()
    for copy in copies:
        copy.wait()


def interior(
    inter_ref, ramp_ref, x_ref, near_ref, w_ref, gamma_ref, bias_ref,
    out_hbm, part_ref, last_ref, carry_ref, nacc_ref,
    line, flat, nflat, acc, done_s, o_sem,
):
    frames, rows, width, chans = x_ref.shape
    depth = TAPS * chans // LANES
    passes = conv_passes(depth)
    _, below_first, below_second, _ = scales(inter_ref, ramp_ref)
    below = (below_first, below_second)
    gamma = 0.5 * gamma_ref[...]
    clear_ends(line)
    near_kh = 2 * (1 - parity())

    def flat_at(f, h):
        return last_ref.at[h] if f == frames - 1 else flat.at[f, h]

    queue = Queue()
    ready = {}
    for f in range(frames):
        for h in reversed(range(rows)):
            ready[f, h] = queue.add(
                prepare(x_ref.at[f, h], gamma, line.at[h], flat_at(f, h)))
        ready[f] = queue.add(prepare(near_ref.at[f], gamma, line.at[rows], nflat.at[f]))

    def weight(tile, places):
        return cells(w_ref, tile, places)

    def contribute(g, r, lanes, term, first, final):
        if first:
            term = term + (x_ref[g, r, :, lanes].astype(F32) + bias_ref[:, lanes])
        else:
            term = term + acc[g, r, :, lanes]
        if not final:
            acc[g, r, :, lanes] = term
        elif r == 0:
            part_ref[g, 0, :, lanes] = term
        elif r == rows - 1:
            part_ref[g, 1, :, lanes] = term
        else:
            done_s[g, r - 1, :, lanes] = term.astype(BF16)

    def run(*accs):
        units = Units(accs)

        def pop(f, m, tile, number, r, last):
            product = units.pop(m, number)
            for i, (slot, block) in enumerate(tile):
                lanes = slice(block * LANES, (block + 1) * LANES)
                term = product[:, i * LANES : (i + 1) * LANES]
                if number >= 4:
                    term = term * below[r]
                contribute(
                    f + slot, r, lanes, term,
                    (f == 0 or slot == 2) and number < 4, slot == 0 and last)

        def near(f, job):
            queue.until(ready[f])
            for places in in_pairs([(near_kh, c) for c in range(depth)]):
                low, high = places[0][1] * LANES, (places[-1][1] + 1) * LANES
                for m, (tile, _) in enumerate(job):
                    if m == 0 or tile is not job[0][0]:
                        units.weights(m, cells(w_ref, tile, places))
                        block = nflat[f, :, low:high]
                        units.add(m, 0, block if len(places) == 2 else beside([block]))

        def near_pop(f, job):
            for m, (tile, _) in enumerate(job):
                if m == 0 or tile is not job[0][0]:
                    product = units.pop(m, 0)
                    for i, (slot, block) in enumerate(tile):
                        lanes = slice(block * LANES, (block + 1) * LANES)
                        term = product[:, i * LANES : (i + 1) * LANES]
                        if f > 0 and slot < 2:
                            term = term + nacc_ref[f + slot, :, lanes]
                        nacc_ref[f + slot, :, lanes] = term

        queue.until(ready[0, 0])
        for f in range(frames - 1):
            jobs = jobs_of(tiles_of(chans, min(TAPS, frames - f)), rows)
            for place, job in enumerate(jobs):
                flat_row = lambda h: flat.at[f, h]
                queue.until(ready[f] if f else 0)
                matrix_job(
                    units, job, passes, rows, flat_row, weight,
                    lambda: queue.some(2), lambda *rest: pop(f, *rest),
                    lambda: near(f, job))
                near_pop(f, job)
            copy = pltpu.make_async_copy(
                done_s.at[f], out_hbm.at[f, pl.ds(1, rows - 2)], o_sem.at[f])
            copy.start()
        f = frames - 1
        queue.until(ready[f])
        tiles = tiles_of(chans, 1)
        job = [(tile, None) for tile in tiles]
        near(f, job)
        near_pop(f, job)
        for r in range(rows):
            carry_ref[r] = acc[f, r]
        for f in range(frames - 1):
            pltpu.make_async_copy(
                done_s.at[f], out_hbm.at[f, pl.ds(1, rows - 2)], o_sem.at[f]).wait()

    pl.run_scoped(run, *[pltpu.ACC(m)((width, SIDE), F32) for m in range(MXUS) for _ in range(ACCS)])


def edges(
    inter_ref, ramp_ref, far_ref, w_ref, gamma_ref, part_ref, last_ref, carry_ref, nacc_ref, _,
    out_hbm,
    line, fflat, acc, facc, tail, done_s, inner_s, o_sem, i_sem,
):
    frames, width, chans = far_ref.shape
    rows = out_hbm.shape[1]
    depth = TAPS * chans // LANES
    passes = conv_passes(depth)
    odd = parity()
    top, below_first, below_second, bottom = scales(inter_ref, ramp_ref)
    below = (below_first, below_second)
    far_scale = jnp.where(odd == 1, bottom, top)
    near_scale = jnp.where(odd == 1, top, bottom)
    gamma = 0.5 * gamma_ref[...]
    clear_ends(line)
    final = frames - 1
    blocks = [slice(b * LANES, (b + 1) * LANES) for b in range(chans // LANES)]

    queue = Queue()
    ready = [
        queue.add(prepare(far_ref.at[f], gamma, line.at[0], fflat.at[f])) for f in range(frames)
    ]

    def near_row(g, at):
        span = slice(at, at + CHUNK)
        for lanes in blocks:
            base = tail[1 - odd, span, lanes] if g == final else part_ref[g, 1 - odd, span, lanes]
            total = base + near_scale * nacc_ref[g, span, lanes]
            done_s[g, 1 - odd, span, lanes] = total.astype(BF16)

    def run(*accs):
        units = Units(accs)

        def pop(m, tile, number, r, last):
            product = units.pop(m, number)
            for i, (_, block) in enumerate(tile):
                lanes = blocks[block]
                term = product[:, i * LANES : (i + 1) * LANES]
                if number >= 4:
                    term = acc[r, :, lanes] + term * below[r]
                else:
                    term = carry_ref[r, :, lanes] + term
                if not last:
                    acc[r, :, lanes] = term
                elif r == 0 or r == rows - 1:
                    tail[0 if r == 0 else 1, :, lanes] = term
                else:
                    inner_s[r - 1, :, lanes] = term.astype(BF16)

        tiles = tiles_of(chans, 1)
        job = [(tile, range(rows)) for tile in tiles]
        matrix_job(
            units, job, passes, rows, lambda h: last_ref.at[h],
            lambda tile, places: cells(w_ref, tile, places), lambda: queue.some(2), pop)
        inner = pltpu.make_async_copy(
            inner_s, out_hbm.at[final, pl.ds(1, rows - 2)], i_sem)
        inner.start()
        nears, copies = [], []
        for g in range(frames):
            nears.append(queue.add([lambda g=g, at=at: near_row(g, at) for at in range(0, width, CHUNK)]))
        whole = [
            (f, tile) for f in range(frames) for tile in tiles_of(chans, min(TAPS, frames - f))
        ]
        for number, pair in enumerate(in_pairs(whole)):
            queue.until(ready[max(f for f, _ in pair)])
            here = (number % 2) * 3
            for places in in_pairs([(2 * odd, c) for c in range(depth)]):
                low, high = places[0][1] * LANES, (places[-1][1] + 1) * LANES
                for m, (f, tile) in enumerate(pair):
                    units.weights(m, cells(w_ref, tile, places))
                for m, (f, tile) in enumerate(pair):
                    block = fflat[f, :, low:high]
                    units.add(m, here, block if len(places) == 2 else beside([block]))
                queue.some(1)
            for m, (f, tile) in enumerate(pair):
                product = units.pop(m, here)
                for i, (slot, block) in enumerate(tile):
                    g = f + slot
                    lanes = blocks[block]
                    term = product[:, i * LANES : (i + 1) * LANES]
                    if f > 0 and slot < 2:
                        term = term + facc[g, :, lanes]
                    if slot > 0:
                        facc[g, :, lanes] = term
                        continue
                    base = tail[odd, :, lanes] if g == final else part_ref[g, odd, :, lanes]
                    done_s[g, odd, :, lanes] = (base + far_scale * term).astype(BF16)
                    if block == len(blocks) - 1:
                        queue.until(nears[g])
                        for side in range(2):
                            copies.append(pltpu.make_async_copy(
                                done_s.at[g, side], out_hbm.at[g, side * (rows - 1)],
                                o_sem.at[g, side]))
                            copies[-1].start()
        inner.wait()
        for copy in copies:
            copy.wait()

    pl.run_scoped(run, *[pltpu.ACC(m)((width, SIDE), F32) for m in range(MXUS) for _ in range(ACCS)])


def per_device(latents, gamma, weight, bias, intersection, ramp):
    frames, rows, width, chans = latents.shape
    deep = TAPS * chans
    gamma = gamma.reshape(1, chans)
    bias = bias.reshape(1, chans)
    weight = weight.reshape(TAPS, TAPS, deep, chans)
    count = lax.axis_size("rows")
    smem = pl.BlockSpec(memory_space=pltpu.SMEM)
    vmem = pl.BlockSpec(memory_space=pltpu.VMEM)
    hbm = pl.BlockSpec(memory_space=pltpu.HBM)
    anywhere = pl.BlockSpec(memory_space=pl.ANY)
    dma = pltpu.SemaphoreType.DMA
    inside = lambda array: pltpu.with_memory_space_constraint(array, pltpu.VMEM)
    outside = lambda array: pltpu.with_memory_space_constraint(array, pltpu.HBM)
    swap = lambda array, start: lax.ppermute(array, "rows", [
        pair for k in range(start, count - 1, 2) for pair in ((k, k + 1), (k + 1, k))])
    halo = pltpu.VMEM((frames, width, chans), BF16)
    far, near = pl.pallas_call(
        select,
        out_shape=(halo, halo),
        in_specs=[hbm],
        out_specs=(vmem, vmem),
        scratch_shapes=[dma((2,))],
        cost_estimate=pl.CostEstimate(flops=20 * 10**9, bytes_accessed=4 * 2**20, transcendentals=0),
        compiler_params=pltpu.CompilerParams(vmem_limit_bytes=2**20),
        name="select",
    )(outside(latents))
    weight = inside(weight)
    near = swap(near, 0)
    far = swap(far, 1)
    out, part, last, carry, nacc = pl.pallas_call(
        interior,
        out_shape=(
            jax.ShapeDtypeStruct(latents.shape, BF16),
            pltpu.VMEM((frames - 1, 2, width, chans), F32),
            pltpu.VMEM((rows, width, deep), BF16),
            pltpu.VMEM((rows, width, chans), F32),
            pltpu.VMEM((frames, width, chans), F32),
        ),
        in_specs=[smem, smem, vmem, vmem, vmem, vmem, vmem],
        out_specs=(anywhere,) + (vmem,) * 4,
        scratch_shapes=[
            pltpu.VMEM((rows + 1, width + 16, chans), F32),
            pltpu.VMEM((frames - 1, rows, width, deep), BF16),
            pltpu.VMEM((frames, width, deep), BF16),
            pltpu.VMEM((frames, rows, width, chans), F32),
            pltpu.VMEM((frames - 1, rows - 2, width, chans), BF16),
            dma((frames - 1,)),
        ],
        cost_estimate=pl.CostEstimate(
            flops=2 * 84 * width * deep * chans, bytes_accessed=14 * 2**20, transcendentals=0
        ),
        compiler_params=pltpu.CompilerParams(vmem_limit_bytes=24 * 2**20),
        name="interior",
    )(intersection, ramp, inside(latents), inside(near), weight, gamma, bias)
    return pl.pallas_call(
        edges,
        out_shape=jax.ShapeDtypeStruct(latents.shape, BF16),
        in_specs=[smem, smem] + [vmem] * 7 + [anywhere],
        out_specs=anywhere,
        input_output_aliases={9: 0},
        scratch_shapes=[
            pltpu.VMEM((1, width + 16, chans), F32),
            pltpu.VMEM((frames, width, deep), BF16),
            pltpu.VMEM((rows, width, chans), F32),
            pltpu.VMEM((frames, width, chans), F32),
            pltpu.VMEM((2, width, chans), F32),
            pltpu.VMEM((frames, 2, width, chans), BF16),
            pltpu.VMEM((rows - 2, width, chans), BF16),
            dma((frames, 2)),
            dma(()),
        ],
        cost_estimate=pl.CostEstimate(
            flops=2 * 24 * width * deep * chans, bytes_accessed=4 * 2**20, transcendentals=0
        ),
        compiler_params=pltpu.CompilerParams(vmem_limit_bytes=16 * 2**20),
        name="edges",
    )(
        intersection, ramp, inside(far), weight, gamma, inside(part), inside(last),
        inside(carry), inside(nacc), out,
    )


def solution(mesh):
    in_specs = (P("clips", "rows", None, None), P(), P(), P(), P("clips"), P("clips"))
    out_specs = P("clips", "rows", None, None)
    return jax.shard_map(
        per_device, mesh=mesh, in_specs=in_specs, out_specs=out_specs, check_vma=False
    )
```

```python
import jax
import jax.numpy as jnp
from jax import lax
from jax.experimental import pallas as pl
from jax.experimental.pallas import tpu as pltpu
from jax.sharding import PartitionSpec as P

F32 = jnp.float32
BF16 = jnp.bfloat16
TAPS = 3
LANES = 128
SIDE = 256
RATE = 0.3
CHUNK = 80
MXUS = 2
ACCS = 6


def scales(inter_ref, ramp_ref):
    index = lax.axis_index("rows")
    count = lax.axis_size("rows")
    previous = jnp.maximum(index - 1, 0)
    own = jnp.where(index == count - 1, 0, inter_ref[index])
    before = jnp.where(index > 0, inter_ref[previous], 0)
    row = lambda scalar: jnp.full((1, LANES), scalar, jnp.int32)
    own, before, ramp = row(own), row(before), row(ramp_ref[previous])
    steps = (ramp + 1).astype(F32)
    first = jnp.where(before > 0, jnp.maximum(ramp, 0).astype(F32) / steps, 0.0)
    second = jnp.where(before > 1, jnp.maximum(ramp - 1, 0).astype(F32) / steps, 0.0)
    below_first = jnp.where(before > 1, 1.0, 1.0 - first)
    bottom = jnp.where(own > 0, 1.0, 0.0)
    return first, below_first, 1.0 - second, bottom


def parity():
    return lax.rem(lax.axis_index("rows"), 2)


def activate(values, half_gamma):
    square = jnp.mean(values * values, axis=-1, keepdims=True)
    half = values * lax.rsqrt(square + 1e-06) * half_gamma
    return half + half * jnp.tanh(half)


def prepare(source, gamma, line, target):
    width, chans = source.shape

    def first(at):
        act = activate(source[at : at + CHUNK].astype(F32), gamma)
        for block in range(chans // LANES):
            line[block, 8 + at : 8 + at + CHUNK] = act[:, block * LANES : (block + 1) * LANES]
        target[at : at + CHUNK, chans : 2 * chans] = act.astype(BF16)

    def second(at):
        for step in (0, 2):
            for block in range(chans // LANES):
                piece = line[block, 7 + step + at : 7 + step + at + CHUNK]
                low = step * chans + block * LANES
                target[at : at + CHUNK, low : low + LANES] = piece.astype(BF16)

    for at in range(0, width, CHUNK):
        yield lambda at=at: first(at)
    for at in range(0, width, CHUNK):
        yield lambda at=at: second(at)


def clear_ends(line):
    lines, blocks, padded, lanes = line.shape
    line[:, :, 0:8] = jnp.zeros((lines, blocks, 8, lanes), F32)
    line[:, :, padded - 8 : padded] = jnp.zeros((lines, blocks, 8, lanes), F32)


class Queue:
    def __init__(self):
        self.items = []
        self.done = 0
        self.credit = 0.0

    def add(self, steps):
        self.items.extend(steps)
        return len(self.items)

    def until(self, mark):
        while self.done < mark:
            self.items[self.done]()
            self.done += 1

    def some(self, number):
        self.credit += number
        whole = int(self.credit)
        self.credit -= whole
        self.until(min(len(self.items), self.done + whole))


def tiles_of(chans, count):
    blocks = [(slot, block) for slot in range(count) for block in range(chans // LANES)]
    return [blocks[i : i + 2] for i in range(0, len(blocks), 2)]


def jobs_of(tiles, rows):
    full = range(rows)
    jobs = [
        [(tiles[i], full), (tiles[i + 1], full)] for i in range(0, len(tiles) - 1, 2)
    ]
    if len(tiles) % 2 and len(tiles[-1]) > 1:
        jobs.append([(tiles[-1], full[: rows // 2]), (tiles[-1], full[rows // 2 :])])
    return jobs


def in_pairs(chunks):
    return [chunks[i : i + 2] for i in range(0, len(chunks), 2)]


def cells(w_ref, tile, places):
    columns = []
    for slot, block in tile:
        parts = [
            w_ref[TAPS - 1 - slot, kh, rest * LANES : (rest + 1) * LANES,
                  block * LANES : (block + 1) * LANES]
            for kh, rest in places
        ]
        while len(parts) < 2:
            parts.append(jnp.zeros((LANES, LANES), BF16))
        columns.append(jnp.concatenate(parts, axis=0))
    while len(columns) < 2:
        columns.append(jnp.zeros((SIDE, LANES), BF16))
    return jnp.concatenate(columns, axis=1)


def beside(parts):
    while len(parts) < 2:
        parts = parts + [jnp.zeros_like(parts[0])]
    return jnp.concatenate(parts, axis=1)


class Units:
    def __init__(self, accs):
        self.accs = [accs[m * ACCS : (m + 1) * ACCS] for m in range(MXUS)]
        self.stage = [0] * MXUS
        self.load = [None] * MXUS

    def weights(self, m, operand):
        pltpu.matmul_push_rhs(operand, self.stage[m], m)
        self.load[m] = self.stage[m]
        self.stage[m] = 1 - self.stage[m]

    def add(self, m, number, block):
        pltpu.matmul_acc_lhs(self.accs[m][number], block, self.load[m])
        self.load[m] = None

    def pop(self, m, number):
        return pltpu.matmul_pop(self.accs[m][number])


def conv_passes(depth):
    return in_pairs([divmod(chunk, depth) for chunk in range(TAPS * depth)])


def acc_of(r, places, rows):
    if not any(0 <= r + kh - 1 < rows for kh, _ in places):
        return None
    if r < 2 and places[-1][0] == 2:
        return 4 + r
    return r


def row_block(flat_row, r, places):
    parts = []
    for kh, rest in places:
        h = r + kh - 1
        if h < 0:
            parts.append(jnp.zeros((flat_row(0).shape[0], LANES), BF16))
        else:
            parts.append(flat_row(h)[:, rest * LANES : (rest + 1) * LANES])
    return beside(parts)


def matrix_job(units, job, passes, rows, flat_row, weight, step, pop, between=None):
    for number, places in enumerate(passes):
        active = [
            (m, tile, [r for r in rows_of if acc_of(r, places, rows) is not None])
            for m, (tile, rows_of) in enumerate(job)
        ]
        for m, tile, rows_of in active:
            if rows_of:
                units.weights(m, weight(tile, places))
        for r in (3, 1, 2, 0):
            if any(r in rows_of for _, _, rows_of in active):
                block = row_block(flat_row, r, places)
                for m, _, rows_of in active:
                    if r in rows_of:
                        units.add(m, acc_of(r, places, rows), block)
                step()
        if between is not None and number == len(passes) - 3:
            between()
        for r in (3, 1, 0, 2):
            here = acc_of(r, places, rows)
            later = [acc_of(r, other, rows) for other in passes[number + 1 :]]
            if here is not None and here not in later:
                last = all(other is None for other in later)
                for m, (tile, rows_of) in enumerate(job):
                    if r in rows_of:
                        pop(m, tile, here, r, last)


def crossed(w_ref, slot, block, khs, chunks):
    columns = []
    for kh in khs:
        parts = [
            w_ref[TAPS - 1 - slot, kh, rest * LANES : (rest + 1) * LANES,
                  block * LANES : (block + 1) * LANES]
            for rest in chunks
        ]
        while len(parts) < 2:
            parts.append(jnp.zeros((LANES, LANES), BF16))
        columns.append(jnp.concatenate(parts, axis=0))
    return jnp.concatenate(columns, axis=1)


def crossed_terms(rows):
    middle = rows // 2
    upper = [
        (h, [(0, h + 1, 0)] + ([(1, h, 1)] if h < middle else [])) for h in range(rows - 1)
    ]
    lower = [
        (h, [(0, h - 1, 2)] + ([(1, h, 1)] if h >= middle else [])) for h in range(1, rows)
    ]
    return upper, lower


def crossed_steps(units, m, part, numbers, w_ref, slot, block, depth, rows, flat_row):
    khs = ((0, 1), (2, 1))[part]
    heights = [h for h, _ in crossed_terms(rows)[part]]
    for chunks in in_pairs(range(depth)):
        yield 0, lambda chunks=chunks: units.weights(
            m, crossed(w_ref, slot, block, khs, chunks))
        for h in heights:
            yield 1, lambda chunks=chunks, h=h: units.add(m, numbers[h], beside(
                [flat_row(h)[:, c * LANES : (c + 1) * LANES] for c in chunks]))


def crossed_pops(units, places, rows, give):
    items = []
    for part, (m, numbers) in enumerate(places):
        for h, uses in crossed_terms(rows)[part]:
            items.append((m, numbers[h], uses))
    order = [r for _, _, uses in items for _, r, _ in uses]
    seen = 0
    for m, number, uses in items:
        product = units.pop(m, number)
        for half, r, kh in uses:
            term = product[:, half * LANES : (half + 1) * LANES]
            give(r, kh, term, r not in order[:seen], r not in order[seen + 1 :])
            seen += 1


def merged(streams, step):
    streams = [list(stream) for stream in streams]
    totals = [max(1, sum(cost for cost, _ in stream)) for stream in streams]
    spent = [0] * len(streams)
    while any(streams):
        live = [i for i, stream in enumerate(streams) if stream]
        i = min(live, key=lambda i: spent[i] / totals[i])
        cost, run = streams[i].pop(0)
        run()
        spent[i] += cost
        if cost:
            step()


def select(x_hbm, far_ref, near_ref, sem):
    frames, rows = x_hbm.shape[:2]
    odd = parity()
    copies = []
    for place, (target, row) in enumerate(
        ((far_ref, odd * (rows - 1)), (near_ref, (1 - odd) * (rows - 1)))
    ):
        copies.append(pltpu.make_async_copy(x_hbm.at[:, row], target, sem.at[place]))
        copies[-1].start()
    for copy in copies:
        copy.wait()


def interior(
    inter_ref, ramp_ref, x_ref, near_ref, w_ref, gamma_ref, bias_ref,
    out_hbm, part_ref, last_ref, carry_ref, nacc_ref, late_ref,
    line, flat, nflat, acc, done_s, o_sem,
):
    frames, rows, width, chans = x_ref.shape
    depth = TAPS * chans // LANES
    passes = conv_passes(depth)
    _, below_first, below_second, _ = scales(inter_ref, ramp_ref)
    below = (below_first, below_second)
    gamma = 0.5 * gamma_ref[...]
    clear_ends(line)
    near_kh = 2 * (1 - parity())

    def flat_at(f, h):
        return last_ref.at[h] if f == frames - 1 else flat.at[f, h]

    queue = Queue()
    ready = {}
    for f in range(frames):
        for h in reversed(range(rows)):
            ready[f, h] = queue.add(
                prepare(x_ref.at[f, h], gamma, line.at[h], flat_at(f, h)))
        ready[f] = queue.add(prepare(near_ref.at[f], gamma, line.at[rows], nflat.at[f]))

    def weight(tile, places):
        return cells(w_ref, tile, places)

    def contribute(g, r, lanes, term, first, final):
        total, at = (carry_ref, (r,)) if g == frames - 1 else (acc, (g, r))
        at = at + (slice(None), lanes)
        if first:
            term = term + (x_ref[g, r, :, lanes].astype(F32) + bias_ref[:, lanes])
        else:
            term = term + total[at]
        if not final:
            total[at] = term
        elif r == 0:
            part_ref[g, 0, :, lanes] = term
        elif r == rows - 1:
            part_ref[g, 1, :, lanes] = term
        elif g == frames - 2:
            late_ref[r - 1, :, lanes] = term.astype(BF16)
        else:
            done_s[g, r - 1, :, lanes] = term.astype(BF16)

    def run(*accs):
        units = Units(accs)

        def pop(f, m, tile, number, r, last):
            product = units.pop(m, number)
            for i, (slot, block) in enumerate(tile):
                lanes = slice(block * LANES, (block + 1) * LANES)
                term = product[:, i * LANES : (i + 1) * LANES]
                if number >= 4:
                    term = term * below[r]
                contribute(
                    f + slot, r, lanes, term,
                    (f == 0 or slot == 2) and number < 4, slot == 0 and last)

        whole = [
            (f, tile) for f in range(frames) for tile in tiles_of(chans, min(TAPS, frames - f))
        ]
        slots = in_pairs(whole)

        def near(slot_pair, number=0):
            for f, _ in slot_pair:
                queue.until(ready[f])
            for places in in_pairs([(near_kh, c) for c in range(depth)]):
                low, high = places[0][1] * LANES, (places[-1][1] + 1) * LANES
                for m, (f, tile) in enumerate(slot_pair):
                    units.weights(m, cells(w_ref, tile, places))
                for m, (f, tile) in enumerate(slot_pair):
                    block = nflat[f, :, low:high]
                    units.add(m, number, block if len(places) == 2 else beside([block]))

        def near_pop(slot_pair, number=0):
            for m, (f, tile) in enumerate(slot_pair):
                product = units.pop(m, number)
                for i, (slot, block) in enumerate(tile):
                    lanes = slice(block * LANES, (block + 1) * LANES)
                    term = product[:, i * LANES : (i + 1) * LANES]
                    if f > 0 and slot < 2:
                        term = term + nacc_ref[f + slot, :, lanes]
                    nacc_ref[f + slot, :, lanes] = term

        queue.until(ready[0, 0])
        copies = []
        for f in range(frames - 1):
            jobs = jobs_of(tiles_of(chans, min(TAPS, frames - f)), rows)
            for place, job in enumerate(jobs):
                flat_row = lambda h: flat.at[f, h]
                if f:
                    queue.until(ready[f, 0])
                here = slots.pop(0)
                matrix_job(
                    units, job, passes, rows, flat_row, weight,
                    lambda: queue.some(RATE), lambda *rest: pop(f, *rest),
                    lambda: near(here))
                near_pop(here)
            tile = tiles_of(chans, min(TAPS, frames - f))[-1]
            if len(tile) == 1:
                (slot, block), here = tile[0], slots.pop(0)
                numbers = {h: h for h in range(rows)}
                flat_row = lambda h: flat.at[f, h]
                merged([
                    crossed_steps(
                        units, part, part, numbers, w_ref, slot, block, depth, rows, flat_row)
                    for part in range(MXUS)
                ], lambda: queue.some(RATE))
                near(here, 4)

                def give(r, kh, term, first, last):
                    if kh == 2 and r < 2:
                        term = term * below[r]
                    contribute(
                        f + slot, r, slice(block * LANES, (block + 1) * LANES), term,
                        first and (f == 0 or slot == 2), last and slot == 0)

                crossed_pops(units, [(0, numbers), (1, numbers)], rows, give)
                near_pop(here, 4)
            if f < frames - 2:
                copies.append(pltpu.make_async_copy(
                    done_s.at[f], out_hbm.at[f, pl.ds(1, rows - 2)], o_sem.at[f]))
                copies[-1].start()
        for here in slots:
            near(here)
            near_pop(here)
        for copy in copies:
            copy.wait()

    pl.run_scoped(run, *[pltpu.ACC(m)((width, SIDE), F32) for m in range(MXUS) for _ in range(ACCS)])


def edges(
    inter_ref, ramp_ref, far_ref, w_ref, gamma_ref, part_ref, last_ref, carry_ref, nacc_ref, late_ref, _,
    out_hbm,
    line, fflat, acc, facc, tail, done_s, inner_s, o_sem, i_sem, l_sem,
):
    frames, width, chans = far_ref.shape
    rows = out_hbm.shape[1]
    depth = TAPS * chans // LANES
    passes = conv_passes(depth)
    odd = parity()
    top, below_first, below_second, bottom = scales(inter_ref, ramp_ref)
    below = (below_first, below_second)
    far_scale = jnp.where(odd == 1, bottom, top)
    near_scale = jnp.where(odd == 1, top, bottom)
    gamma = 0.5 * gamma_ref[...]
    clear_ends(line)
    final = frames - 1
    late = pltpu.make_async_copy(late_ref, out_hbm.at[final - 1, pl.ds(1, rows - 2)], l_sem)
    late.start()
    blocks = [slice(b * LANES, (b + 1) * LANES) for b in range(chans // LANES)]

    queue = Queue()
    ready = [
        queue.add(prepare(far_ref.at[f], gamma, line.at[0], fflat.at[f])) for f in range(frames)
    ]

    def near_row(g, at):
        span = slice(at, at + CHUNK)
        for lanes in blocks:
            base = tail[1 - odd, span, lanes] if g == final else part_ref[g, 1 - odd, span, lanes]
            total = base + near_scale * nacc_ref[g, span, lanes]
            done_s[g, 1 - odd, span, lanes] = total.astype(BF16)

    def run(*accs):
        units = Units(accs)

        def contribute(r, lanes, term, first, last):
            term = term + (carry_ref if first else acc)[r, :, lanes]
            if not last:
                acc[r, :, lanes] = term
            elif r == 0 or r == rows - 1:
                tail[0 if r == 0 else 1, :, lanes] = term
            else:
                inner_s[r - 1, :, lanes] = term.astype(BF16)

        def pop(m, tile, number, r, kept, last):
            product = units.pop(m, number)
            for i, (_, block) in enumerate(tile):
                term = product[:, i * LANES : (i + 1) * LANES]
                contribute(r, blocks[block], term * below[r] if kept else term, not kept, last)

        def taps(m, tile, rows_of, numbers):
            for number, places in enumerate(passes):
                active = [r for r in rows_of if acc_of(r, places, rows) is not None]
                if active:
                    yield 0, lambda places=places: units.weights(m, cells(w_ref, tile, places))
                for r in active:
                    yield 1, lambda r=r, places=places: units.add(
                        m, numbers[acc_of(r, places, rows)], row_block(flat_row, r, places))
                for r in active:
                    here = acc_of(r, places, rows)
                    later = [acc_of(r, other, rows) for other in passes[number + 1 :]]
                    if here not in later:
                        yield 0, lambda r=r, here=here, last=all(o is None for o in later): pop(
                            m, tile, numbers[here], r, here >= rows, last)

        flat_row = lambda h: last_ref.at[h]
        first_tile, rest = tiles_of(chans, 1)
        (_, block), = rest
        upper = {h: h for h in range(rows)}
        lower = {h: 2 + h for h in range(rows)}

        def give(r, kh, term, first, last):
            contribute(r, blocks[block], term * below[r] if kh == 2 and r < 2 else term, first, last)

        def second():
            for part, numbers in enumerate((upper, lower)):
                yield from crossed_steps(
                    units, 1, part, numbers, w_ref, 0, block, depth, rows, flat_row)
            yield 0, lambda: crossed_pops(units, [(1, upper), (1, lower)], rows, give)
            yield from taps(1, first_tile, [0], {0: 0, 4: 1})

        merged(
            [taps(0, first_tile, [3, 1, 2], {r: r for r in range(ACCS)}), second()],
            lambda: queue.some(RATE))
        inner = pltpu.make_async_copy(
            inner_s, out_hbm.at[final, pl.ds(1, rows - 2)], i_sem)
        inner.start()
        nears, copies = [], []
        for g in range(frames):
            nears.append(queue.add([lambda g=g, at=at: near_row(g, at) for at in range(0, width, CHUNK)]))
        whole = [
            (f, tile) for f in range(frames) for tile in tiles_of(chans, min(TAPS, frames - f))
        ]
        for number, pair in enumerate(in_pairs(whole)):
            queue.until(ready[max(f for f, _ in pair)])
            here = (number % 2) * 3
            for places in in_pairs([(2 * odd, c) for c in range(depth)]):
                low, high = places[0][1] * LANES, (places[-1][1] + 1) * LANES
                for m, (f, tile) in enumerate(pair):
                    units.weights(m, cells(w_ref, tile, places))
                for m, (f, tile) in enumerate(pair):
                    block = fflat[f, :, low:high]
                    units.add(m, here, block if len(places) == 2 else beside([block]))
                queue.some(1)
            for m, (f, tile) in enumerate(pair):
                product = units.pop(m, here)
                for i, (slot, block) in enumerate(tile):
                    g = f + slot
                    lanes = blocks[block]
                    term = product[:, i * LANES : (i + 1) * LANES]
                    if f > 0 and slot < 2:
                        term = term + facc[g, :, lanes]
                    if slot > 0:
                        facc[g, :, lanes] = term
                        continue
                    base = tail[odd, :, lanes] if g == final else part_ref[g, odd, :, lanes]
                    done_s[g, odd, :, lanes] = (base + far_scale * term).astype(BF16)
                    if block == len(blocks) - 1:
                        queue.until(nears[g])
                        for side in range(2):
                            copies.append(pltpu.make_async_copy(
                                done_s.at[g, side], out_hbm.at[g, side * (rows - 1)],
                                o_sem.at[g, side]))
                            copies[-1].start()
        inner.wait()
        for copy in copies:
            copy.wait()
        late.wait()

    pl.run_scoped(run, *[pltpu.ACC(m)((width, SIDE), F32) for m in range(MXUS) for _ in range(ACCS)])


def per_device(latents, gamma, weight, bias, intersection, ramp):
    frames, rows, width, chans = latents.shape
    deep = TAPS * chans
    gamma = gamma.reshape(1, chans)
    bias = bias.reshape(1, chans)
    weight = weight.reshape(TAPS, TAPS, deep, chans)
    count = lax.axis_size("rows")
    smem = pl.BlockSpec(memory_space=pltpu.SMEM)
    vmem = pl.BlockSpec(memory_space=pltpu.VMEM)
    hbm = pl.BlockSpec(memory_space=pltpu.HBM)
    anywhere = pl.BlockSpec(memory_space=pl.ANY)
    dma = pltpu.SemaphoreType.DMA
    inside = lambda array: pltpu.with_memory_space_constraint(array, pltpu.VMEM)
    outside = lambda array: pltpu.with_memory_space_constraint(array, pltpu.HBM)
    swap = lambda array, start: lax.ppermute(array, "rows", [
        pair for k in range(start, count - 1, 2) for pair in ((k, k + 1), (k + 1, k))])
    halo = pltpu.VMEM((frames, width, chans), BF16)
    far, near = pl.pallas_call(
        select,
        out_shape=(halo, halo),
        in_specs=[hbm],
        out_specs=(vmem, vmem),
        scratch_shapes=[dma((2,))],
        cost_estimate=pl.CostEstimate(flops=20 * 10**9, bytes_accessed=4 * 2**20, transcendentals=0),
        compiler_params=pltpu.CompilerParams(vmem_limit_bytes=2**20),
        name="select",
    )(outside(latents))
    weight = inside(weight)
    near = swap(near, 0)
    far = swap(far, 1)
    out, part, last, carry, nacc, late = pl.pallas_call(
        interior,
        out_shape=(
            jax.ShapeDtypeStruct(latents.shape, BF16),
            pltpu.VMEM((frames - 1, 2, width, chans), F32),
            pltpu.VMEM((rows, width, deep), BF16),
            pltpu.VMEM((rows, width, chans), F32),
            pltpu.VMEM((frames, width, chans), F32),
            pltpu.VMEM((rows - 2, width, chans), BF16),
        ),
        in_specs=[smem, smem, vmem, vmem, vmem, vmem, vmem],
        out_specs=(anywhere,) + (vmem,) * 5,
        scratch_shapes=[
            pltpu.VMEM((rows + 1, chans // LANES, width + 16, LANES), F32),
            pltpu.VMEM((frames - 1, rows, width, deep), BF16),
            pltpu.VMEM((frames, width, deep), BF16),
            pltpu.VMEM((frames - 1, rows, width, chans), F32),
            pltpu.VMEM((frames - 2, rows - 2, width, chans), BF16),
            dma((frames - 2,)),
        ],
        cost_estimate=pl.CostEstimate(
            flops=2 * 84 * width * deep * chans, bytes_accessed=14 * 2**20, transcendentals=0
        ),
        compiler_params=pltpu.CompilerParams(vmem_limit_bytes=24 * 2**20),
        name="interior",
    )(intersection, ramp, inside(latents), inside(near), weight, gamma, bias)
    return pl.pallas_call(
        edges,
        out_shape=jax.ShapeDtypeStruct(latents.shape, BF16),
        in_specs=[smem, smem] + [vmem] * 8 + [anywhere],
        out_specs=anywhere,
        input_output_aliases={10: 0},
        scratch_shapes=[
            pltpu.VMEM((1, chans // LANES, width + 16, LANES), F32),
            pltpu.VMEM((frames, width, deep), BF16),
            pltpu.VMEM((rows, width, chans), F32),
            pltpu.VMEM((frames, width, chans), F32),
            pltpu.VMEM((2, width, chans), F32),
            pltpu.VMEM((frames, 2, width, chans), BF16),
            pltpu.VMEM((rows - 2, width, chans), BF16),
            dma((frames, 2)),
            dma(()),
            dma(()),
        ],
        cost_estimate=pl.CostEstimate(
            flops=2 * 24 * width * deep * chans, bytes_accessed=4 * 2**20, transcendentals=0
        ),
        compiler_params=pltpu.CompilerParams(vmem_limit_bytes=16 * 2**20),
        name="edges",
    )(
        intersection, ramp, inside(far), weight, gamma, inside(part), inside(last),
        inside(carry), inside(nacc), inside(late), out,
    )


def solution(mesh):
    in_specs = (P("clips", "rows", None, None), P(), P(), P(), P("clips"), P("clips"))
    out_specs = P("clips", "rows", None, None)
    return jax.shard_map(
        per_device, mesh=mesh, in_specs=in_specs, out_specs=out_specs, check_vma=False
    )
```

```python
import jax
import jax.numpy as jnp
from jax import lax
from jax.experimental import pallas as pl
from jax.experimental.pallas import tpu as pltpu
from jax.sharding import PartitionSpec as P

F32 = jnp.float32
BF16 = jnp.bfloat16
TAPS = 3
LANES = 128
SIDE = 256
RATE = 0.4
CHUNK = 80
MXUS = 2
ACCS = 6


def scales(inter_ref, ramp_ref):
    index = lax.axis_index("rows")
    count = lax.axis_size("rows")
    previous = jnp.maximum(index - 1, 0)
    own = jnp.where(index == count - 1, 0, inter_ref[index])
    before = jnp.where(index > 0, inter_ref[previous], 0)
    row = lambda scalar: jnp.full((1, LANES), scalar, jnp.int32)
    own, before, ramp = row(own), row(before), row(ramp_ref[previous])
    steps = (ramp + 1).astype(F32)
    first = jnp.where(before > 0, jnp.maximum(ramp, 0).astype(F32) / steps, 0.0)
    second = jnp.where(before > 1, jnp.maximum(ramp - 1, 0).astype(F32) / steps, 0.0)
    below_first = jnp.where(before > 1, 1.0, 1.0 - first)
    bottom = jnp.where(own > 0, 1.0, 0.0)
    return first, below_first, 1.0 - second, bottom


def parity():
    return lax.rem(lax.axis_index("rows"), 2)


def activate(values, half_gamma):
    square = jnp.mean(values * values, axis=-1, keepdims=True)
    half = values * lax.rsqrt(square + 1e-06) * half_gamma
    return half + half * jnp.tanh(half)


def prepare(source, gamma, line, target):
    width, chans = source.shape

    def first(at):
        act = activate(source[at : at + CHUNK].astype(F32), gamma)
        for block in range(chans // LANES):
            line[block, 8 + at : 8 + at + CHUNK] = act[:, block * LANES : (block + 1) * LANES]
        target[at : at + CHUNK, chans : 2 * chans] = act.astype(BF16)

    def second(at):
        for step in (0, 2):
            for block in range(chans // LANES):
                piece = line[block, 7 + step + at : 7 + step + at + CHUNK]
                low = step * chans + block * LANES
                target[at : at + CHUNK, low : low + LANES] = piece.astype(BF16)

    for at in range(0, width, CHUNK):
        yield lambda at=at: first(at)
    for at in range(0, width, CHUNK):
        yield lambda at=at: second(at)


def clear_ends(line):
    lines, blocks, padded, lanes = line.shape
    line[:, :, 0:8] = jnp.zeros((lines, blocks, 8, lanes), F32)
    line[:, :, padded - 8 : padded] = jnp.zeros((lines, blocks, 8, lanes), F32)


class Queue:
    def __init__(self):
        self.items = []
        self.done = 0
        self.credit = 0.0

    def add(self, steps):
        self.items.extend(steps)
        return len(self.items)

    def until(self, mark):
        while self.done < mark:
            self.items[self.done]()
            self.done += 1

    def some(self, number):
        self.credit += number
        whole = int(self.credit)
        self.credit -= whole
        self.until(min(len(self.items), self.done + whole))


def tiles_of(chans, count):
    blocks = [(slot, block) for slot in range(count) for block in range(chans // LANES)]
    return [blocks[i : i + 2] for i in range(0, len(blocks), 2)]


def jobs_of(tiles, rows):
    full = range(rows)
    jobs = [
        [(tiles[i], full), (tiles[i + 1], full)] for i in range(0, len(tiles) - 1, 2)
    ]
    if len(tiles) % 2 and len(tiles[-1]) > 1:
        jobs.append([(tiles[-1], full[: rows // 2]), (tiles[-1], full[rows // 2 :])])
    return jobs


def in_pairs(chunks):
    return [chunks[i : i + 2] for i in range(0, len(chunks), 2)]


def cells(w_ref, tile, places):
    columns = []
    for slot, block in tile:
        parts = [
            w_ref[TAPS - 1 - slot, kh, rest * LANES : (rest + 1) * LANES,
                  block * LANES : (block + 1) * LANES]
            for kh, rest in places
        ]
        while len(parts) < 2:
            parts.append(jnp.zeros((LANES, LANES), BF16))
        columns.append(jnp.concatenate(parts, axis=0))
    while len(columns) < 2:
        columns.append(jnp.zeros((SIDE, LANES), BF16))
    return jnp.concatenate(columns, axis=1)


def beside(parts):
    while len(parts) < 2:
        parts = parts + [jnp.zeros_like(parts[0])]
    return jnp.concatenate(parts, axis=1)


class Units:
    def __init__(self, accs):
        self.accs = [accs[m * ACCS : (m + 1) * ACCS] for m in range(MXUS)]
        self.stage = [0] * MXUS
        self.load = [None] * MXUS

    def weights(self, m, operand):
        pltpu.matmul_push_rhs(operand, self.stage[m], m)
        self.load[m] = self.stage[m]
        self.stage[m] = 1 - self.stage[m]

    def add(self, m, number, block):
        pltpu.matmul_acc_lhs(self.accs[m][number], block, self.load[m])
        self.load[m] = None

    def pop(self, m, number):
        return pltpu.matmul_pop(self.accs[m][number])


def conv_passes(depth):
    return in_pairs([divmod(chunk, depth) for chunk in range(TAPS * depth)])


def acc_of(r, places, rows):
    if not any(0 <= r + kh - 1 < rows for kh, _ in places):
        return None
    if r < 2 and places[-1][0] == 2:
        return 4 + r
    return r


def row_block(flat_row, r, places):
    parts = []
    for kh, rest in places:
        h = r + kh - 1
        if h < 0:
            parts.append(jnp.zeros((flat_row(0).shape[0], LANES), BF16))
        else:
            parts.append(flat_row(h)[:, rest * LANES : (rest + 1) * LANES])
    return beside(parts)


def matrix_job(units, job, passes, rows, flat_row, weight, step, pop):
    for number, places in enumerate(passes):
        active = [
            (m, tile, [r for r in rows_of if acc_of(r, places, rows) is not None])
            for m, (tile, rows_of) in enumerate(job)
        ]
        for m, tile, rows_of in active:
            if rows_of:
                units.weights(m, weight(tile, places))
        for r in (3, 1, 2, 0):
            if any(r in rows_of for _, _, rows_of in active):
                block = row_block(flat_row, r, places)
                for m, _, rows_of in active:
                    if r in rows_of:
                        units.add(m, acc_of(r, places, rows), block)
                step()
        for r in (3, 1, 0, 2):
            here = acc_of(r, places, rows)
            later = [acc_of(r, other, rows) for other in passes[number + 1 :]]
            if here is not None and here not in later:
                last = all(other is None for other in later)
                for m, (tile, rows_of) in enumerate(job):
                    if r in rows_of:
                        pop(m, tile, here, r, last)


def crossed(w_ref, slot, block, khs, chunks):
    columns = []
    for kh in khs:
        parts = [
            w_ref[TAPS - 1 - slot, kh, rest * LANES : (rest + 1) * LANES,
                  block * LANES : (block + 1) * LANES]
            for rest in chunks
        ]
        while len(parts) < 2:
            parts.append(jnp.zeros((LANES, LANES), BF16))
        columns.append(jnp.concatenate(parts, axis=0))
    return jnp.concatenate(columns, axis=1)


def crossed_terms(rows):
    middle = rows // 2
    upper = [
        (h, [(0, h + 1, 0)] + ([(1, h, 1)] if h < middle else [])) for h in range(rows - 1)
    ]
    lower = [
        (h, [(0, h - 1, 2)] + ([(1, h, 1)] if h >= middle else [])) for h in range(1, rows)
    ]
    return upper, lower


def crossed_steps(units, m, part, numbers, w_ref, slot, block, depth, rows, flat_row):
    khs = ((0, 1), (2, 1))[part]
    heights = [h for h, _ in crossed_terms(rows)[part]]
    for chunks in in_pairs(range(depth)):
        yield 0, lambda chunks=chunks: units.weights(
            m, crossed(w_ref, slot, block, khs, chunks))
        for h in heights:
            yield 1, lambda chunks=chunks, h=h: units.add(m, numbers[h], beside(
                [flat_row(h)[:, c * LANES : (c + 1) * LANES] for c in chunks]))


def crossed_pops(units, places, rows, give):
    items = []
    for part, (m, numbers) in enumerate(places):
        for h, uses in crossed_terms(rows)[part]:
            items.append((m, numbers[h], uses))
    order = [r for _, _, uses in items for _, r, _ in uses]
    seen = 0
    for m, number, uses in items:
        product = units.pop(m, number)
        for half, r, kh in uses:
            term = product[:, half * LANES : (half + 1) * LANES]
            give(r, kh, term, r not in order[:seen], r not in order[seen + 1 :])
            seen += 1


def halo_jobs(frames, depth):
    run = lambda f, slots: [(f, chunk, slots) for chunk in range(depth)]
    wide = [
        (sum((run(f, (g - f, g - f)) for f in range(max(0, g + 1 - TAPS), g + 1)), []), (0, 1), (g, g))
        for g in range(frames)
    ]
    thin = [(run(f, (0, 1)), (2, 2), (f, f + 1)) for f in range(frames - 1)]
    alone = {}
    for f, slot in [(f, 2) for f in range(frames - 2)] + [(frames - 1, 0)]:
        alone[f + slot] = alone.get(f + slot, []) + run(f, (slot,))
    second = wide[:1] + thin
    for g, entries in alone.items():
        second.append((entries, (2,), (g,)))
    second.sort(key=lambda job: (max(f for f, _, _ in job[0]), len(job[1]) < 2))
    return wide[1:], second


def halo_steps(units, m, jobs, w_ref, kh, flat_ref, give):
    for number, (entries, blocks, made) in enumerate(jobs):
        number = number % ACCS
        for pair in in_pairs(entries):
            def operand(pair=pair, blocks=blocks):
                columns = []
                for j, block in enumerate(blocks):
                    parts = [
                        w_ref[TAPS - 1 - slots[j], kh, chunk * LANES : (chunk + 1) * LANES,
                              block * LANES : (block + 1) * LANES]
                        for _, chunk, slots in pair
                    ]
                    while len(parts) < 2:
                        parts.append(jnp.zeros((LANES, LANES), BF16))
                    columns.append(jnp.concatenate(parts, axis=0))
                while len(columns) < 2:
                    columns.append(jnp.zeros((SIDE, LANES), BF16))
                units.weights(m, jnp.concatenate(columns, axis=1))

            def multiply(pair=pair, number=number):
                units.add(m, number, beside([
                    flat_ref[f, :, chunk * LANES : (chunk + 1) * LANES] for f, chunk, _ in pair]))

            yield 0, operand
            yield 1, multiply

        def hand(number=number, blocks=blocks, made=made):
            product = units.pop(m, number)
            for j, (block, g) in enumerate(zip(blocks, made)):
                give(g, block, product[:, j * LANES : (j + 1) * LANES])

        yield 0, hand


def halo_shares(frames, depth):
    shares = {}
    for jobs in halo_jobs(frames, depth):
        for _, blocks, made in jobs:
            for key in zip(made, blocks):
                shares[key] = shares.get(key, 0) + 1
    return shares


def merged(streams, step):
    streams = [list(stream) for stream in streams]
    totals = [max(1, sum(cost for cost, _ in stream)) for stream in streams]
    spent = [0] * len(streams)
    while any(streams):
        live = [i for i, stream in enumerate(streams) if stream]
        i = min(live, key=lambda i: spent[i] / totals[i])
        cost, run = streams[i].pop(0)
        run()
        spent[i] += cost
        if cost:
            step()


def select(x_hbm, far_ref, near_ref, sem):
    frames, rows = x_hbm.shape[:2]
    odd = parity()
    copies = []
    for place, (target, row) in enumerate(
        ((far_ref, odd * (rows - 1)), (near_ref, (1 - odd) * (rows - 1)))
    ):
        copies.append(pltpu.make_async_copy(x_hbm.at[:, row], target, sem.at[place]))
        copies[-1].start()
    for copy in copies:
        copy.wait()


def interior(
    inter_ref, ramp_ref, x_ref, near_ref, w_ref, gamma_ref, bias_ref,
    out_hbm, part_ref, last_ref, carry_ref, nacc_ref, late_ref,
    line, flat, nflat, acc, done_s, o_sem,
):
    frames, rows, width, chans = x_ref.shape
    depth = TAPS * chans // LANES
    passes = conv_passes(depth)
    _, below_first, below_second, _ = scales(inter_ref, ramp_ref)
    below = (below_first, below_second)
    gamma = 0.5 * gamma_ref[...]
    clear_ends(line)
    near_kh = 2 * (1 - parity())

    def flat_at(f, h):
        return last_ref.at[h] if f == frames - 1 else flat.at[f, h]

    queue = Queue()
    ready = {}
    for f in range(frames):
        for h in reversed(range(rows)):
            ready[f, h] = queue.add(
                prepare(x_ref.at[f, h], gamma, line.at[h], flat_at(f, h)))
        ready[f] = queue.add(prepare(near_ref.at[f], gamma, line.at[rows], nflat.at[f]))

    def weight(tile, places):
        return cells(w_ref, tile, places)

    def contribute(g, r, lanes, term, first, final):
        total, at = (carry_ref, (r,)) if g == frames - 1 else (acc, (g, r))
        at = at + (slice(None), lanes)
        if first:
            term = term + (x_ref[g, r, :, lanes].astype(F32) + bias_ref[:, lanes])
        else:
            term = term + total[at]
        if not final:
            total[at] = term
        elif r == 0:
            part_ref[g, 0, :, lanes] = term
        elif r == rows - 1:
            part_ref[g, 1, :, lanes] = term
        elif g == frames - 2:
            late_ref[r - 1, :, lanes] = term.astype(BF16)
        else:
            done_s[g, r - 1, :, lanes] = term.astype(BF16)

    def run(*accs):
        units = Units(accs)

        def pop(f, m, tile, number, r, last):
            product = units.pop(m, number)
            for i, (slot, block) in enumerate(tile):
                lanes = slice(block * LANES, (block + 1) * LANES)
                term = product[:, i * LANES : (i + 1) * LANES]
                if number >= 4:
                    term = term * below[r]
                contribute(
                    f + slot, r, lanes, term,
                    (f == 0 or slot == 2) and number < 4, slot == 0 and last)

        queue.until(ready[0, 0])
        copies = []
        for f in range(frames - 1):
            jobs = jobs_of(tiles_of(chans, min(TAPS, frames - f)), rows)
            for place, job in enumerate(jobs):
                flat_row = lambda h: flat.at[f, h]
                if f:
                    queue.until(ready[f, 0])
                matrix_job(
                    units, job, passes, rows, flat_row, weight,
                    lambda: queue.some(RATE), lambda *rest: pop(f, *rest))
            tile = tiles_of(chans, min(TAPS, frames - f))[-1]
            if len(tile) == 1:
                (slot, block), = tile
                numbers = {h: h for h in range(rows)}
                flat_row = lambda h: flat.at[f, h]
                merged([
                    crossed_steps(
                        units, part, part, numbers, w_ref, slot, block, depth, rows, flat_row)
                    for part in range(MXUS)
                ], lambda: queue.some(RATE))

                def give(r, kh, term, first, last):
                    if kh == 2 and r < 2:
                        term = term * below[r]
                    contribute(
                        f + slot, r, slice(block * LANES, (block + 1) * LANES), term,
                        first and (f == 0 or slot == 2), last and slot == 0)

                crossed_pops(units, [(0, numbers), (1, numbers)], rows, give)
            if f < frames - 2:
                copies.append(pltpu.make_async_copy(
                    done_s.at[f], out_hbm.at[f, pl.ds(1, rows - 2)], o_sem.at[f]))
                copies[-1].start()
        queue.until(len(queue.items))
        seen = set()

        def near(g, block, term):
            lanes = slice(block * LANES, (block + 1) * LANES)
            if (g, block) in seen:
                term = term + nacc_ref[g, :, lanes]
            seen.add((g, block))
            nacc_ref[g, :, lanes] = term

        merged([
            halo_steps(units, m, jobs, w_ref, near_kh, nflat, near)
            for m, jobs in enumerate(halo_jobs(frames, depth))
        ], lambda: None)
        for copy in copies:
            copy.wait()

    pl.run_scoped(run, *[pltpu.ACC(m)((width, SIDE), F32) for m in range(MXUS) for _ in range(ACCS)])


def edges(
    inter_ref, ramp_ref, far_ref, w_ref, gamma_ref, part_ref, last_ref, carry_ref, nacc_ref, late_ref, _,
    out_hbm,
    line, fflat, acc, facc, tail, done_s, inner_s, o_sem, i_sem, l_sem,
):
    frames, width, chans = far_ref.shape
    rows = out_hbm.shape[1]
    depth = TAPS * chans // LANES
    passes = conv_passes(depth)
    odd = parity()
    top, below_first, below_second, bottom = scales(inter_ref, ramp_ref)
    below = (below_first, below_second)
    far_scale = jnp.where(odd == 1, bottom, top)
    near_scale = jnp.where(odd == 1, top, bottom)
    gamma = 0.5 * gamma_ref[...]
    clear_ends(line)
    final = frames - 1
    late = pltpu.make_async_copy(late_ref, out_hbm.at[final - 1, pl.ds(1, rows - 2)], l_sem)
    late.start()
    blocks = [slice(b * LANES, (b + 1) * LANES) for b in range(chans // LANES)]

    queue = Queue()
    ready = [
        queue.add(prepare(far_ref.at[f], gamma, line.at[0], fflat.at[f])) for f in range(frames)
    ]

    def near_row(g, at):
        span = slice(at, at + CHUNK)
        for lanes in blocks:
            base = tail[1 - odd, span, lanes] if g == final else part_ref[g, 1 - odd, span, lanes]
            total = base + near_scale * nacc_ref[g, span, lanes]
            done_s[g, 1 - odd, span, lanes] = total.astype(BF16)

    def run(*accs):
        units = Units(accs)

        def contribute(r, lanes, term, first, last):
            term = term + (carry_ref if first else acc)[r, :, lanes]
            if not last:
                acc[r, :, lanes] = term
            elif r == 0 or r == rows - 1:
                tail[0 if r == 0 else 1, :, lanes] = term
            else:
                inner_s[r - 1, :, lanes] = term.astype(BF16)

        def pop(m, tile, number, r, kept, last):
            product = units.pop(m, number)
            for i, (_, block) in enumerate(tile):
                term = product[:, i * LANES : (i + 1) * LANES]
                contribute(r, blocks[block], term * below[r] if kept else term, not kept, last)

        def taps(m, tile, rows_of, numbers):
            for number, places in enumerate(passes):
                active = [r for r in rows_of if acc_of(r, places, rows) is not None]
                if active:
                    yield 0, lambda places=places: units.weights(m, cells(w_ref, tile, places))
                for r in active:
                    yield 1, lambda r=r, places=places: units.add(
                        m, numbers[acc_of(r, places, rows)], row_block(flat_row, r, places))
                for r in active:
                    here = acc_of(r, places, rows)
                    later = [acc_of(r, other, rows) for other in passes[number + 1 :]]
                    if here not in later:
                        yield 0, lambda r=r, here=here, last=all(o is None for o in later): pop(
                            m, tile, numbers[here], r, here >= rows, last)

        flat_row = lambda h: last_ref.at[h]
        first_tile, rest = tiles_of(chans, 1)
        (_, block), = rest
        upper = {h: h for h in range(rows)}
        lower = {h: 2 + h for h in range(rows)}

        def give(r, kh, term, first, last):
            contribute(r, blocks[block], term * below[r] if kh == 2 and r < 2 else term, first, last)

        def second():
            for part, numbers in enumerate((upper, lower)):
                yield from crossed_steps(
                    units, 1, part, numbers, w_ref, 0, block, depth, rows, flat_row)
            yield 0, lambda: crossed_pops(units, [(1, upper), (1, lower)], rows, give)
            yield from taps(1, first_tile, [0], {0: 0, 4: 1})

        merged(
            [taps(0, first_tile, [3, 1, 2], {r: r for r in range(ACCS)}), second()],
            lambda: queue.some(RATE))
        inner = pltpu.make_async_copy(
            inner_s, out_hbm.at[final, pl.ds(1, rows - 2)], i_sem)
        inner.start()
        nears, copies = [], []
        for g in range(frames):
            nears.append(queue.add([lambda g=g, at=at: near_row(g, at) for at in range(0, width, CHUNK)]))
        queue.until(ready[-1])
        shares = halo_shares(frames, depth)
        seen = {}

        def give(g, block, term):
            lanes = blocks[block]
            seen[g, block] = seen.get((g, block), 0) + 1
            if seen[g, block] > 1:
                term = term + facc[g, :, lanes]
            if seen[g, block] < shares[g, block]:
                facc[g, :, lanes] = term
                return
            base = tail[odd, :, lanes] if g == final else part_ref[g, odd, :, lanes]
            done_s[g, odd, :, lanes] = (base + far_scale * term).astype(BF16)
            if all(seen.get((g, b)) == shares[g, b] for b in range(len(blocks))):
                queue.until(nears[g])
                for side in range(2):
                    copies.append(pltpu.make_async_copy(
                        done_s.at[g, side], out_hbm.at[g, side * (rows - 1)],
                        o_sem.at[g, side]))
                    copies[-1].start()

        merged([
            halo_steps(units, m, jobs, w_ref, 2 * odd, fflat, give)
            for m, jobs in enumerate(halo_jobs(frames, depth))
        ], lambda: queue.some(1))
        inner.wait()
        for copy in copies:
            copy.wait()
        late.wait()

    pl.run_scoped(run, *[pltpu.ACC(m)((width, SIDE), F32) for m in range(MXUS) for _ in range(ACCS)])


def per_device(latents, gamma, weight, bias, intersection, ramp):
    frames, rows, width, chans = latents.shape
    deep = TAPS * chans
    gamma = gamma.reshape(1, chans)
    bias = bias.reshape(1, chans)
    weight = weight.reshape(TAPS, TAPS, deep, chans)
    count = lax.axis_size("rows")
    smem = pl.BlockSpec(memory_space=pltpu.SMEM)
    vmem = pl.BlockSpec(memory_space=pltpu.VMEM)
    hbm = pl.BlockSpec(memory_space=pltpu.HBM)
    anywhere = pl.BlockSpec(memory_space=pl.ANY)
    dma = pltpu.SemaphoreType.DMA
    inside = lambda array: pltpu.with_memory_space_constraint(array, pltpu.VMEM)
    outside = lambda array: pltpu.with_memory_space_constraint(array, pltpu.HBM)
    swap = lambda array, start: lax.ppermute(array, "rows", [
        pair for k in range(start, count - 1, 2) for pair in ((k, k + 1), (k + 1, k))])
    halo = pltpu.VMEM((frames, width, chans), BF16)
    far, near = pl.pallas_call(
        select,
        out_shape=(halo, halo),
        in_specs=[hbm],
        out_specs=(vmem, vmem),
        scratch_shapes=[dma((2,))],
        cost_estimate=pl.CostEstimate(flops=20 * 10**9, bytes_accessed=4 * 2**20, transcendentals=0),
        compiler_params=pltpu.CompilerParams(vmem_limit_bytes=2**20),
        name="select",
    )(outside(latents))
    weight = inside(weight)
    near = swap(near, 0)
    far = swap(far, 1)
    out, part, last, carry, nacc, late = pl.pallas_call(
        interior,
        out_shape=(
            jax.ShapeDtypeStruct(latents.shape, BF16),
            pltpu.VMEM((frames - 1, 2, width, chans), F32),
            pltpu.VMEM((rows, width, deep), BF16),
            pltpu.VMEM((rows, width, chans), F32),
            pltpu.VMEM((frames, width, chans), F32),
            pltpu.VMEM((rows - 2, width, chans), BF16),
        ),
        in_specs=[smem, smem, vmem, vmem, vmem, vmem, vmem],
        out_specs=(anywhere,) + (vmem,) * 5,
        scratch_shapes=[
            pltpu.VMEM((rows + 1, chans // LANES, width + 16, LANES), F32),
            pltpu.VMEM((frames - 1, rows, width, deep), BF16),
            pltpu.VMEM((frames, width, deep), BF16),
            pltpu.VMEM((frames - 1, rows, width, chans), F32),
            pltpu.VMEM((frames - 2, rows - 2, width, chans), BF16),
            dma((frames - 2,)),
        ],
        cost_estimate=pl.CostEstimate(
            flops=2 * 84 * width * deep * chans, bytes_accessed=14 * 2**20, transcendentals=0
        ),
        compiler_params=pltpu.CompilerParams(vmem_limit_bytes=24 * 2**20),
        name="interior",
    )(intersection, ramp, inside(latents), inside(near), weight, gamma, bias)
    return pl.pallas_call(
        edges,
        out_shape=jax.ShapeDtypeStruct(latents.shape, BF16),
        in_specs=[smem, smem] + [vmem] * 8 + [anywhere],
        out_specs=anywhere,
        input_output_aliases={10: 0},
        scratch_shapes=[
            pltpu.VMEM((1, chans // LANES, width + 16, LANES), F32),
            pltpu.VMEM((frames, width, deep), BF16),
            pltpu.VMEM((rows, width, chans), F32),
            pltpu.VMEM((frames, width, chans), F32),
            pltpu.VMEM((2, width, chans), F32),
            pltpu.VMEM((frames, 2, width, chans), BF16),
            pltpu.VMEM((rows - 2, width, chans), BF16),
            dma((frames, 2)),
            dma(()),
            dma(()),
        ],
        cost_estimate=pl.CostEstimate(
            flops=2 * 24 * width * deep * chans, bytes_accessed=4 * 2**20, transcendentals=0
        ),
        compiler_params=pltpu.CompilerParams(vmem_limit_bytes=16 * 2**20),
        name="edges",
    )(
        intersection, ramp, inside(far), weight, gamma, inside(part), inside(last),
        inside(carry), inside(nacc), inside(late), out,
    )


def solution(mesh):
    in_specs = (P("clips", "rows", None, None), P(), P(), P(), P("clips"), P("clips"))
    out_specs = P("clips", "rows", None, None)
    return jax.shard_map(
        per_device, mesh=mesh, in_specs=in_specs, out_specs=out_specs, check_vma=False
    )
```

```python
import itertools

import jax
import jax.numpy as jnp
from jax import lax
from jax.experimental import pallas as pl
from jax.experimental.pallas import tpu as pltpu
from jax.sharding import PartitionSpec as P

F32 = jnp.float32
BF16 = jnp.bfloat16
TAPS = 3
LANES = 128
SIDE = 256
RATE = 0.4
CHUNK = 80
MXUS = 2
ACCS = 6


def scales(inter_ref, ramp_ref):
    index = lax.axis_index("rows")
    count = lax.axis_size("rows")
    previous = jnp.maximum(index - 1, 0)
    own = jnp.where(index == count - 1, 0, inter_ref[index])
    before = jnp.where(index > 0, inter_ref[previous], 0)
    row = lambda scalar: jnp.full((1, LANES), scalar, jnp.int32)
    own, before, ramp = row(own), row(before), row(ramp_ref[previous])
    steps = (ramp + 1).astype(F32)
    first = jnp.where(before > 0, jnp.maximum(ramp, 0).astype(F32) / steps, 0.0)
    second = jnp.where(before > 1, jnp.maximum(ramp - 1, 0).astype(F32) / steps, 0.0)
    below_first = jnp.where(before > 1, 1.0, 1.0 - first)
    bottom = jnp.where(own > 0, 1.0, 0.0)
    return first, below_first, 1.0 - second, bottom


def parity():
    return lax.rem(lax.axis_index("rows"), 2)


def activate(values, half_gamma):
    square = jnp.mean(values * values, axis=-1, keepdims=True)
    half = values * lax.rsqrt(square + 1e-06) * half_gamma
    return half + half * jnp.tanh(half)


def prepare(source, gamma, line, target):
    width, chans = source.shape

    def first(at):
        act = activate(source[at : at + CHUNK].astype(F32), gamma)
        for block in range(chans // LANES):
            line[block, 8 + at : 8 + at + CHUNK] = act[:, block * LANES : (block + 1) * LANES]
        target[at : at + CHUNK, chans : 2 * chans] = act.astype(BF16)

    def second(at):
        for step in (0, 2):
            for block in range(chans // LANES):
                piece = line[block, 7 + step + at : 7 + step + at + CHUNK]
                low = step * chans + block * LANES
                target[at : at + CHUNK, low : low + LANES] = piece.astype(BF16)

    for at in range(0, width, CHUNK):
        yield lambda at=at: first(at)
    for at in range(0, width, CHUNK):
        yield lambda at=at: second(at)


def clear_ends(line):
    lines, blocks, padded, lanes = line.shape
    line[:, :, 0:8] = jnp.zeros((lines, blocks, 8, lanes), F32)
    line[:, :, padded - 8 : padded] = jnp.zeros((lines, blocks, 8, lanes), F32)


class Queue:
    def __init__(self):
        self.items = []
        self.done = 0
        self.credit = 0.0

    def add(self, steps):
        self.items.extend(steps)
        return len(self.items)

    def until(self, mark):
        while self.done < mark:
            self.items[self.done]()
            self.done += 1

    def some(self, number):
        self.credit += number
        whole = int(self.credit)
        self.credit -= whole
        self.until(min(len(self.items), self.done + whole))


def tiles_of(chans, count):
    blocks = [(slot, block) for slot in range(count) for block in range(chans // LANES)]
    return [blocks[i : i + 2] for i in range(0, len(blocks), 2)]


def jobs_of(tiles, rows):
    full = range(rows)
    jobs = [
        [(tiles[i], full), (tiles[i + 1], full)] for i in range(0, len(tiles) - 1, 2)
    ]
    if len(tiles) % 2 and len(tiles[-1]) > 1:
        jobs.append([(tiles[-1], full[: rows // 2]), (tiles[-1], full[rows // 2 :])])
    return jobs


def in_pairs(chunks):
    return [chunks[i : i + 2] for i in range(0, len(chunks), 2)]


def cells(w_ref, tile, places):
    columns = []
    for slot, block in tile:
        parts = [
            w_ref[TAPS - 1 - slot, kh, rest * LANES : (rest + 1) * LANES,
                  block * LANES : (block + 1) * LANES]
            for kh, rest in places
        ]
        while len(parts) < 2:
            parts.append(jnp.zeros((LANES, LANES), BF16))
        columns.append(jnp.concatenate(parts, axis=0))
    while len(columns) < 2:
        columns.append(jnp.zeros((SIDE, LANES), BF16))
    return jnp.concatenate(columns, axis=1)


def beside(parts):
    while len(parts) < 2:
        parts = parts + [jnp.zeros_like(parts[0])]
    return jnp.concatenate(parts, axis=1)


class Units:
    def __init__(self, accs):
        self.accs = [accs[m * ACCS : (m + 1) * ACCS] for m in range(MXUS)]
        self.stage = [0] * MXUS
        self.load = [None] * MXUS

    def weights(self, m, operand):
        pltpu.matmul_push_rhs(operand, self.stage[m], m)
        self.load[m] = self.stage[m]
        self.stage[m] = 1 - self.stage[m]

    def add(self, m, number, block):
        pltpu.matmul_acc_lhs(self.accs[m][number], block, self.load[m])
        self.load[m] = None

    def pop(self, m, number):
        return pltpu.matmul_pop(self.accs[m][number])


def conv_passes(depth):
    return in_pairs([divmod(chunk, depth) for chunk in range(TAPS * depth)])


def acc_of(r, places, rows):
    if not any(0 <= r + kh - 1 < rows for kh, _ in places):
        return None
    if r < 2 and places[-1][0] == 2:
        return 4 + r
    return r


def row_block(flat_row, r, places):
    parts = []
    for kh, rest in places:
        h = r + kh - 1
        if h < 0:
            parts.append(jnp.zeros((flat_row(0).shape[0], LANES), BF16))
        else:
            parts.append(flat_row(h)[:, rest * LANES : (rest + 1) * LANES])
    return beside(parts)


def matrix_job(units, job, passes, rows, flat_row, weight, step, pop):
    for number, places in enumerate(passes):
        active = [
            (m, tile, [r for r in rows_of if acc_of(r, places, rows) is not None])
            for m, (tile, rows_of) in enumerate(job)
        ]
        for m, tile, rows_of in active:
            if rows_of:
                units.weights(m, weight(tile, places))
        for r in (3, 1, 2, 0):
            if any(r in rows_of for _, _, rows_of in active):
                block = row_block(flat_row, r, places)
                for m, _, rows_of in active:
                    if r in rows_of:
                        units.add(m, acc_of(r, places, rows), block)
                step()
        for r in (3, 1, 0, 2):
            here = acc_of(r, places, rows)
            later = [acc_of(r, other, rows) for other in passes[number + 1 :]]
            if here is not None and here not in later:
                last = all(other is None for other in later)
                for m, (tile, rows_of) in enumerate(job):
                    if r in rows_of:
                        pop(m, tile, here, r, last)


def crossed(w_ref, slot, block, khs, chunks):
    columns = []
    for kh in khs:
        parts = [
            w_ref[TAPS - 1 - slot, kh, rest * LANES : (rest + 1) * LANES,
                  block * LANES : (block + 1) * LANES]
            for rest in chunks
        ]
        while len(parts) < 2:
            parts.append(jnp.zeros((LANES, LANES), BF16))
        columns.append(jnp.concatenate(parts, axis=0))
    return jnp.concatenate(columns, axis=1)


def crossed_terms(rows):
    middle = rows // 2
    upper = [
        (h, [(0, h + 1, 0)] + ([(1, h, 1)] if h < middle else [])) for h in range(rows - 1)
    ]
    lower = [
        (h, [(0, h - 1, 2)] + ([(1, h, 1)] if h >= middle else [])) for h in range(1, rows)
    ]
    return upper, lower


def crossed_steps(units, m, part, numbers, w_ref, slot, block, depth, rows, flat_row):
    khs = ((0, 1), (2, 1))[part]
    heights = [h for h, _ in crossed_terms(rows)[part]]
    for chunks in in_pairs(range(depth)):
        yield 0, lambda chunks=chunks: units.weights(
            m, crossed(w_ref, slot, block, khs, chunks))
        for h in heights:
            yield 1, lambda chunks=chunks, h=h: units.add(m, numbers[h], beside(
                [flat_row(h)[:, c * LANES : (c + 1) * LANES] for c in chunks]))


def crossed_pops(units, places, rows, give):
    items = []
    for part, (m, numbers) in enumerate(places):
        for h, uses in crossed_terms(rows)[part]:
            items.append((m, numbers[h], uses))
    order = [r for _, _, uses in items for _, r, _ in uses]
    seen = 0
    for m, number, uses in items:
        product = units.pop(m, number)
        for half, r, kh in uses:
            term = product[:, half * LANES : (half + 1) * LANES]
            give(r, kh, term, r not in order[:seen], r not in order[seen + 1 :])
            seen += 1


def halo_jobs(frames, depth):
    run = lambda f, slots: [(f, chunk, slots) for chunk in range(depth)]
    wide = [
        (sum((run(f, (g - f, g - f)) for f in range(max(0, g + 1 - TAPS), g + 1)), []), (0, 1), (g, g))
        for g in range(frames)
    ]
    thin = [(run(f, (0, 1)), (2, 2), (f, f + 1)) for f in range(frames - 1)]
    alone = {}
    for f, slot in [(f, 2) for f in range(frames - 2)] + [(frames - 1, 0)]:
        alone[f + slot] = alone.get(f + slot, []) + run(f, (slot,))
    second = wide[:1] + thin
    for g, entries in alone.items():
        second.append((entries, (2,), (g,)))
    second.sort(key=lambda job: (max(f for f, _, _ in job[0]), len(job[1]) < 2))
    return wide[1:], second


def halo_steps(units, m, jobs, w_ref, kh, flat_ref, give):
    for number, (entries, blocks, made) in enumerate(jobs):
        number = number % ACCS
        for pair in in_pairs(entries):
            def operand(pair=pair, blocks=blocks):
                columns = []
                for j, block in enumerate(blocks):
                    parts = [
                        w_ref[TAPS - 1 - slots[j], kh, chunk * LANES : (chunk + 1) * LANES,
                              block * LANES : (block + 1) * LANES]
                        for _, chunk, slots in pair
                    ]
                    while len(parts) < 2:
                        parts.append(jnp.zeros((LANES, LANES), BF16))
                    columns.append(jnp.concatenate(parts, axis=0))
                while len(columns) < 2:
                    columns.append(jnp.zeros((SIDE, LANES), BF16))
                units.weights(m, jnp.concatenate(columns, axis=1))

            def multiply(pair=pair, number=number):
                units.add(m, number, beside([
                    flat_ref[f, :, chunk * LANES : (chunk + 1) * LANES] for f, chunk, _ in pair]))

            yield 0, operand
            yield 1, multiply

        def hand(number=number, blocks=blocks, made=made):
            product = units.pop(m, number)
            for j, (block, g) in enumerate(zip(blocks, made)):
                give(g, block, product[:, j * LANES : (j + 1) * LANES])

        yield 0, hand


def halo_shares(frames, depth):
    shares = {}
    for jobs in halo_jobs(frames, depth):
        for _, blocks, made in jobs:
            for key in zip(made, blocks):
                shares[key] = shares.get(key, 0) + 1
    return shares


def merged(streams, step):
    streams = [list(stream) for stream in streams]
    totals = [max(1, sum(cost for cost, _ in stream)) for stream in streams]
    spent = [0] * len(streams)
    while any(streams):
        live = [i for i, stream in enumerate(streams) if stream]
        i = min(live, key=lambda i: spent[i] / totals[i])
        cost, run = streams[i].pop(0)
        run()
        spent[i] += cost
        if cost:
            step()


def select(x_hbm, far_ref, near_ref, sem):
    frames, rows = x_hbm.shape[:2]
    odd = parity()
    copies = []
    for place, (target, row) in enumerate(
        ((far_ref, odd * (rows - 1)), (near_ref, (1 - odd) * (rows - 1)))
    ):
        copies.append(pltpu.make_async_copy(x_hbm.at[:, row], target, sem.at[place]))
        copies[-1].start()
    for copy in copies:
        copy.wait()


def interior(
    inter_ref, ramp_ref, x_ref, near_ref, w_ref, gamma_ref, bias_ref,
    out_hbm, part_ref, last_ref, carry_ref, nacc_ref, late_ref,
    line, flat, nflat, acc, done_s, o_sem,
):
    frames, rows, width, chans = x_ref.shape
    depth = TAPS * chans // LANES
    passes = conv_passes(depth)
    _, below_first, below_second, _ = scales(inter_ref, ramp_ref)
    below = (below_first, below_second)
    gamma = 0.5 * gamma_ref[...]
    clear_ends(line)
    near_kh = 2 * (1 - parity())

    def flat_at(f, h):
        return last_ref.at[h] if f == frames - 1 else flat.at[f, h]

    queue = Queue()
    ready = {}
    for f in range(frames):
        for h in reversed(range(rows)):
            ready[f, h] = queue.add(
                prepare(x_ref.at[f, h], gamma, line.at[h], flat_at(f, h)))
        ready[f] = queue.add(prepare(near_ref.at[f], gamma, line.at[rows], nflat.at[f]))

    def weight(tile, places):
        return cells(w_ref, tile, places)

    def contribute(g, r, lanes, term, first, final):
        total, at = (carry_ref, (r,)) if g == frames - 1 else (acc, (g, r))
        at = at + (slice(None), lanes)
        if first:
            term = term + (x_ref[g, r, :, lanes].astype(F32) + bias_ref[:, lanes])
        else:
            term = term + total[at]
        if not final:
            total[at] = term
        elif r == 0:
            part_ref[g, 0, :, lanes] = term
        elif r == rows - 1:
            part_ref[g, 1, :, lanes] = term
        elif g == frames - 2:
            late_ref[r - 1, :, lanes] = term.astype(BF16)
        else:
            done_s[g, r - 1, :, lanes] = term.astype(BF16)

    def run(*accs):
        units = Units(accs)

        def pop(f, m, tile, number, r, last):
            product = units.pop(m, number)
            for i, (slot, block) in enumerate(tile):
                lanes = slice(block * LANES, (block + 1) * LANES)
                term = product[:, i * LANES : (i + 1) * LANES]
                if number >= 4:
                    term = term * below[r]
                contribute(
                    f + slot, r, lanes, term,
                    (f == 0 or slot == 2) and number < 4, slot == 0 and last)

        queue.until(ready[0, 0])
        copies = []
        for f in range(frames - 1):
            jobs = jobs_of(tiles_of(chans, min(TAPS, frames - f)), rows)
            for place, job in enumerate(jobs):
                flat_row = lambda h: flat.at[f, h]
                if f:
                    queue.until(ready[f, 0])
                matrix_job(
                    units, job, passes, rows, flat_row, weight,
                    lambda: queue.some(RATE), lambda *rest: pop(f, *rest))
            tile = tiles_of(chans, min(TAPS, frames - f))[-1]
            if len(tile) == 1:
                (slot, block), = tile
                numbers = {h: h for h in range(rows)}
                flat_row = lambda h: flat.at[f, h]
                merged([
                    crossed_steps(
                        units, part, part, numbers, w_ref, slot, block, depth, rows, flat_row)
                    for part in range(MXUS)
                ], lambda: queue.some(RATE))

                def give(r, kh, term, first, last):
                    if kh == 2 and r < 2:
                        term = term * below[r]
                    contribute(
                        f + slot, r, slice(block * LANES, (block + 1) * LANES), term,
                        first and (f == 0 or slot == 2), last and slot == 0)

                crossed_pops(units, [(0, numbers), (1, numbers)], rows, give)
            if f < frames - 2:
                copies.append(pltpu.make_async_copy(
                    done_s.at[f], out_hbm.at[f, pl.ds(1, rows - 2)], o_sem.at[f]))
                copies[-1].start()
        queue.until(len(queue.items))
        seen = set()

        def near(g, block, term):
            lanes = slice(block * LANES, (block + 1) * LANES)
            if (g, block) in seen:
                term = term + nacc_ref[g, :, lanes]
            seen.add((g, block))
            nacc_ref[g, :, lanes] = term

        merged([
            halo_steps(units, m, jobs, w_ref, near_kh, nflat, near)
            for m, jobs in enumerate(halo_jobs(frames, depth))
        ], lambda: None)
        for copy in copies:
            copy.wait()

    pl.run_scoped(run, *[pltpu.ACC(m)((width, SIDE), F32) for m in range(MXUS) for _ in range(ACCS)])


def edges(
    inter_ref, ramp_ref, far_ref, w_ref, gamma_ref, part_ref, last_ref, carry_ref, nacc_ref, late_ref, _,
    out_hbm,
    line, fflat, acc, facc, tail, done_s, inner_s, o_sem, i_sem, l_sem,
):
    frames, width, chans = far_ref.shape
    rows = out_hbm.shape[1]
    depth = TAPS * chans // LANES
    passes = conv_passes(depth)
    odd = parity()
    top, below_first, below_second, bottom = scales(inter_ref, ramp_ref)
    below = (below_first, below_second)
    far_scale = jnp.where(odd == 1, bottom, top)
    near_scale = jnp.where(odd == 1, top, bottom)
    gamma = 0.5 * gamma_ref[...]
    clear_ends(line)
    final = frames - 1
    late = pltpu.make_async_copy(late_ref, out_hbm.at[final - 1, pl.ds(1, rows - 2)], l_sem)
    late.start()
    blocks = [slice(b * LANES, (b + 1) * LANES) for b in range(chans // LANES)]

    queue = Queue()
    ready = [
        queue.add(prepare(far_ref.at[f], gamma, line.at[0], fflat.at[f])) for f in range(frames)
    ]

    def near_row(g, at):
        span = slice(at, at + CHUNK)
        for lanes in blocks:
            base = tail[1 - odd, span, lanes] if g == final else part_ref[g, 1 - odd, span, lanes]
            total = base + near_scale * nacc_ref[g, span, lanes]
            done_s[g, 1 - odd, span, lanes] = total.astype(BF16)

    def run(*accs):
        units = Units(accs)

        def contribute(r, lanes, term, first, last):
            term = term + (carry_ref if first else acc)[r, :, lanes]
            if not last:
                acc[r, :, lanes] = term
            elif r == 0 or r == rows - 1:
                tail[0 if r == 0 else 1, :, lanes] = term
            else:
                inner_s[r - 1, :, lanes] = term.astype(BF16)
            if last:
                made.append(r)
                if len(made) == rows * len(blocks):
                    settle()

        def pop(m, tile, number, r, kept, last):
            product = units.pop(m, number)
            for i, (_, block) in enumerate(tile):
                term = product[:, i * LANES : (i + 1) * LANES]
                contribute(r, blocks[block], term * below[r] if kept else term, not kept, last)

        def taps(m, tile, rows_of, numbers):
            for number, places in enumerate(passes):
                active = [r for r in rows_of if acc_of(r, places, rows) is not None]
                if active:
                    yield 0, lambda places=places: units.weights(m, cells(w_ref, tile, places))
                for r in active:
                    yield 1, lambda r=r, places=places: units.add(
                        m, numbers[acc_of(r, places, rows)], row_block(flat_row, r, places))
                for r in active:
                    here = acc_of(r, places, rows)
                    later = [acc_of(r, other, rows) for other in passes[number + 1 :]]
                    if here not in later:
                        yield 0, lambda r=r, here=here, last=all(o is None for o in later): pop(
                            m, tile, numbers[here], r, here >= rows, last)

        flat_row = lambda h: last_ref.at[h]
        first_tile, rest = tiles_of(chans, 1)
        (_, block), = rest
        upper = {h: h for h in range(rows)}
        lower = {h: 2 + h for h in range(rows)}

        def give(r, kh, term, first, last):
            contribute(r, blocks[block], term * below[r] if kh == 2 and r < 2 else term, first, last)

        def second():
            for part, numbers in enumerate((upper, lower)):
                yield from crossed_steps(
                    units, 1, part, numbers, w_ref, 0, block, depth, rows, flat_row)
            yield 0, lambda: crossed_pops(units, [(1, upper), (1, lower)], rows, give)
            yield from taps(1, first_tile, [0], {0: 0, 4: 1})

        copies, made = [], []
        inner = pltpu.make_async_copy(
            inner_s, out_hbm.at[final, pl.ds(1, rows - 2)], i_sem)

        def send(g, kind):
            side = (1 - odd, odd)[kind]
            copies.append(pltpu.make_async_copy(
                done_s.at[g, side], out_hbm.at[g, side * (rows - 1)], o_sem.at[g, kind]))
            copies[-1].start()

        def settle():
            inner.start()
            for g in range(frames):
                queue.add([lambda g=g, at=at: near_row(g, at) for at in range(0, width, CHUNK)])
                queue.add([lambda g=g: send(g, 0)])

        shares = halo_shares(frames, depth)
        seen = {}

        def collect(g, block, term):
            lanes = blocks[block]
            seen[g, block] = seen.get((g, block), 0) + 1
            if seen[g, block] > 1:
                term = term + facc[g, :, lanes]
            if seen[g, block] < shares[g, block]:
                facc[g, :, lanes] = term
                return
            base = tail[odd, :, lanes] if g == final else part_ref[g, odd, :, lanes]
            done_s[g, odd, :, lanes] = (base + far_scale * term).astype(BF16)
            if all(seen.get((g, b)) == shares[g, b] for b in range(len(blocks))):
                send(g, 1)

        def halo(m):
            yield 0, lambda: queue.until(ready[-1])
            yield from halo_steps(
                units, m, halo_jobs(frames, depth)[m], w_ref, 2 * odd, fflat, collect)

        merged([
            itertools.chain(taps(0, first_tile, [3, 1, 2], {r: r for r in range(ACCS)}), halo(0)),
            itertools.chain(second(), halo(1)),
        ], lambda: queue.some(RATE))
        queue.until(len(queue.items))
        inner.wait()
        for copy in copies:
            copy.wait()
        late.wait()

    pl.run_scoped(run, *[pltpu.ACC(m)((width, SIDE), F32) for m in range(MXUS) for _ in range(ACCS)])


def per_device(latents, gamma, weight, bias, intersection, ramp):
    frames, rows, width, chans = latents.shape
    deep = TAPS * chans
    gamma = gamma.reshape(1, chans)
    bias = bias.reshape(1, chans)
    weight = weight.reshape(TAPS, TAPS, deep, chans)
    count = lax.axis_size("rows")
    smem = pl.BlockSpec(memory_space=pltpu.SMEM)
    vmem = pl.BlockSpec(memory_space=pltpu.VMEM)
    hbm = pl.BlockSpec(memory_space=pltpu.HBM)
    anywhere = pl.BlockSpec(memory_space=pl.ANY)
    dma = pltpu.SemaphoreType.DMA
    inside = lambda array: pltpu.with_memory_space_constraint(array, pltpu.VMEM)
    outside = lambda array: pltpu.with_memory_space_constraint(array, pltpu.HBM)
    swap = lambda array, start: lax.ppermute(array, "rows", [
        pair for k in range(start, count - 1, 2) for pair in ((k, k + 1), (k + 1, k))])
    halo = pltpu.VMEM((frames, width, chans), BF16)
    far, near = pl.pallas_call(
        select,
        out_shape=(halo, halo),
        in_specs=[hbm],
        out_specs=(vmem, vmem),
        scratch_shapes=[dma((2,))],
        cost_estimate=pl.CostEstimate(flops=20 * 10**9, bytes_accessed=4 * 2**20, transcendentals=0),
        compiler_params=pltpu.CompilerParams(vmem_limit_bytes=2**20),
        name="select",
    )(outside(latents))
    weight = inside(weight)
    near = swap(near, 0)
    far = swap(far, 1)
    out, part, last, carry, nacc, late = pl.pallas_call(
        interior,
        out_shape=(
            jax.ShapeDtypeStruct(latents.shape, BF16),
            pltpu.VMEM((frames - 1, 2, width, chans), F32),
            pltpu.VMEM((rows, width, deep), BF16),
            pltpu.VMEM((rows, width, chans), F32),
            pltpu.VMEM((frames, width, chans), F32),
            pltpu.VMEM((rows - 2, width, chans), BF16),
        ),
        in_specs=[smem, smem, vmem, vmem, vmem, vmem, vmem],
        out_specs=(anywhere,) + (vmem,) * 5,
        scratch_shapes=[
            pltpu.VMEM((rows + 1, chans // LANES, width + 16, LANES), F32),
            pltpu.VMEM((frames - 1, rows, width, deep), BF16),
            pltpu.VMEM((frames, width, deep), BF16),
            pltpu.VMEM((frames - 1, rows, width, chans), F32),
            pltpu.VMEM((frames - 2, rows - 2, width, chans), BF16),
            dma((frames - 2,)),
        ],
        cost_estimate=pl.CostEstimate(
            flops=2 * 84 * width * deep * chans, bytes_accessed=14 * 2**20, transcendentals=0
        ),
        compiler_params=pltpu.CompilerParams(vmem_limit_bytes=24 * 2**20),
        name="interior",
    )(intersection, ramp, inside(latents), inside(near), weight, gamma, bias)
    return pl.pallas_call(
        edges,
        out_shape=jax.ShapeDtypeStruct(latents.shape, BF16),
        in_specs=[smem, smem] + [vmem] * 8 + [anywhere],
        out_specs=anywhere,
        input_output_aliases={10: 0},
        scratch_shapes=[
            pltpu.VMEM((1, chans // LANES, width + 16, LANES), F32),
            pltpu.VMEM((frames, width, deep), BF16),
            pltpu.VMEM((rows, width, chans), F32),
            pltpu.VMEM((frames, width, chans), F32),
            pltpu.VMEM((2, width, chans), F32),
            pltpu.VMEM((frames, 2, width, chans), BF16),
            pltpu.VMEM((rows - 2, width, chans), BF16),
            dma((frames, 2)),
            dma(()),
            dma(()),
        ],
        cost_estimate=pl.CostEstimate(
            flops=2 * 24 * width * deep * chans, bytes_accessed=4 * 2**20, transcendentals=0
        ),
        compiler_params=pltpu.CompilerParams(vmem_limit_bytes=16 * 2**20),
        name="edges",
    )(
        intersection, ramp, inside(far), weight, gamma, inside(part), inside(last),
        inside(carry), inside(nacc), inside(late), out,
    )


def solution(mesh):
    in_specs = (P("clips", "rows", None, None), P(), P(), P(), P("clips"), P("clips"))
    out_specs = P("clips", "rows", None, None)
    return jax.shard_map(
        per_device, mesh=mesh, in_specs=in_specs, out_specs=out_specs, check_vma=False
    )
```

```python
import itertools

import jax
import jax.numpy as jnp
from jax import lax
from jax.experimental import pallas as pl
from jax.experimental.pallas import tpu as pltpu
from jax.sharding import PartitionSpec as P

F32 = jnp.float32
BF16 = jnp.bfloat16
TAPS = 3
LANES = 128
SIDE = 256
RATE = 1.8
ORDER = (3, 1, 2, 0)
CHUNK = 16
MXUS = 2
ACCS = 6


def scales(inter_ref, ramp_ref):
    index = lax.axis_index("rows")
    count = lax.axis_size("rows")
    previous = jnp.maximum(index - 1, 0)
    own = jnp.where(index == count - 1, 0, inter_ref[index])
    before = jnp.where(index > 0, inter_ref[previous], 0)
    row = lambda scalar: jnp.full((1, LANES), scalar, jnp.int32)
    own, before, ramp = row(own), row(before), row(ramp_ref[previous])
    steps = (ramp + 1).astype(F32)
    first = jnp.where(before > 0, jnp.maximum(ramp, 0).astype(F32) / steps, 0.0)
    second = jnp.where(before > 1, jnp.maximum(ramp - 1, 0).astype(F32) / steps, 0.0)
    below_first = jnp.where(before > 1, 1.0, 1.0 - first)
    bottom = jnp.where(own > 0, 1.0, 0.0)
    return first, below_first, 1.0 - second, bottom


def parity():
    return lax.rem(lax.axis_index("rows"), 2)


def activate(values, half_gamma):
    square = jnp.mean(values * values, axis=-1, keepdims=True)
    half = values * lax.rsqrt(square + 1e-06) * half_gamma
    return half + half * jnp.tanh(half)


def prepare(source, gamma, line, target):
    width, chans = source.shape

    def first(at):
        act = activate(source[at : at + CHUNK].astype(F32), gamma)
        for block in range(chans // LANES):
            line[block, 8 + at : 8 + at + CHUNK] = act[:, block * LANES : (block + 1) * LANES]
        target[at : at + CHUNK, chans : 2 * chans] = act.astype(BF16)

    def second(at):
        for step in (0, 2):
            for block in range(chans // LANES):
                piece = line[block, 7 + step + at : 7 + step + at + CHUNK]
                low = step * chans + block * LANES
                target[at : at + CHUNK, low : low + LANES] = piece.astype(BF16)

    for at in range(0, width, CHUNK):
        yield lambda at=at: first(at)
    for at in range(0, width, CHUNK):
        yield lambda at=at: second(at)


def clear_ends(line):
    lines, blocks, padded, lanes = line.shape
    line[:, :, 0:8] = jnp.zeros((lines, blocks, 8, lanes), F32)
    line[:, :, padded - 8 : padded] = jnp.zeros((lines, blocks, 8, lanes), F32)


class Queue:
    def __init__(self):
        self.items = []
        self.done = 0
        self.credit = 0.0

    def add(self, steps):
        self.items.extend(steps)
        return len(self.items)

    def until(self, mark):
        while self.done < mark:
            self.items[self.done]()
            self.done += 1

    def some(self, number):
        self.credit += number
        whole = int(self.credit)
        self.credit -= whole
        self.until(min(len(self.items), self.done + whole))


def tiles_of(chans, count):
    blocks = [(slot, block) for slot in range(count) for block in range(chans // LANES)]
    return [blocks[i : i + 2] for i in range(0, len(blocks), 2)]


def jobs_of(tiles, rows):
    full = range(rows)
    jobs = [
        [(tiles[i], full), (tiles[i + 1], full)] for i in range(0, len(tiles) - 1, 2)
    ]
    if len(tiles) % 2 and len(tiles[-1]) > 1:
        jobs.append([(tiles[-1], full[: rows // 2]), (tiles[-1], full[rows // 2 :])])
    return jobs


def in_pairs(chunks):
    return [chunks[i : i + 2] for i in range(0, len(chunks), 2)]


def cells(w_ref, tile, places):
    columns = []
    for slot, block in tile:
        parts = [
            w_ref[TAPS - 1 - slot, kh, rest * LANES : (rest + 1) * LANES,
                  block * LANES : (block + 1) * LANES]
            for kh, rest in places
        ]
        while len(parts) < 2:
            parts.append(jnp.zeros((LANES, LANES), BF16))
        columns.append(jnp.concatenate(parts, axis=0))
    while len(columns) < 2:
        columns.append(jnp.zeros((SIDE, LANES), BF16))
    return jnp.concatenate(columns, axis=1)


def beside(parts):
    while len(parts) < 2:
        parts = parts + [jnp.zeros_like(parts[0])]
    return jnp.concatenate(parts, axis=1)


class Units:
    def __init__(self, accs):
        self.accs = [accs[m * ACCS : (m + 1) * ACCS] for m in range(MXUS)]
        self.stage = [0] * MXUS
        self.waiting = [[] for _ in range(MXUS)]

    def weights(self, m, operand):
        pltpu.matmul_push_rhs(operand, self.stage[m], m)
        self.waiting[m].append(self.stage[m])
        self.stage[m] = 1 - self.stage[m]

    def add(self, m, number, block, fresh):
        load = self.waiting[m].pop(0) if fresh else None
        pltpu.matmul_acc_lhs(self.accs[m][number], block, load)

    def pop(self, m, number):
        return pltpu.matmul_pop(self.accs[m][number])


def conv_passes(depth):
    return in_pairs([divmod(chunk, depth) for chunk in range(TAPS * depth)])


def acc_of(r, places, rows):
    if not any(0 <= r + kh - 1 < rows for kh, _ in places):
        return None
    if r < 2 and places[-1][0] == 2:
        return 4 + r
    return r


def row_block(flat_row, r, places):
    parts = []
    for kh, rest in places:
        h = r + kh - 1
        if h < 0:
            parts.append(jnp.zeros((flat_row(0).shape[0], LANES), BF16))
        else:
            parts.append(flat_row(h)[:, rest * LANES : (rest + 1) * LANES])
    return beside(parts)


def matrix_job(units, job, passes, rows, flat_row, weight, step, pop):
    def active(places):
        return [
            (m, tile, [r for r in ORDER if r in rows_of and acc_of(r, places, rows) is not None])
            for m, (tile, rows_of) in enumerate(job)
        ]

    def push(places):
        for m, tile, rows_of in active(places):
            if rows_of:
                units.weights(m, weight(tile, places))

    push(passes[0])
    for number, places in enumerate(passes):
        if number + 1 < len(passes):
            push(passes[number + 1])
        here = active(places)
        for r in ORDER:
            if any(r in rows_of for _, _, rows_of in here):
                block = row_block(flat_row, r, places)
                for m, _, rows_of in here:
                    if r in rows_of:
                        units.add(m, acc_of(r, places, rows), block, r == rows_of[0])
                step()
        for r in (3, 1, 0, 2):
            here = acc_of(r, places, rows)
            later = [acc_of(r, other, rows) for other in passes[number + 1 :]]
            if here is not None and here not in later:
                last = all(other is None for other in later)
                for m, (tile, rows_of) in enumerate(job):
                    if r in rows_of:
                        pop(m, tile, here, r, last)


def crossed(w_ref, slot, block, khs, chunks):
    columns = []
    for kh in khs:
        parts = [
            w_ref[TAPS - 1 - slot, kh, rest * LANES : (rest + 1) * LANES,
                  block * LANES : (block + 1) * LANES]
            for rest in chunks
        ]
        while len(parts) < 2:
            parts.append(jnp.zeros((LANES, LANES), BF16))
        columns.append(jnp.concatenate(parts, axis=0))
    return jnp.concatenate(columns, axis=1)


def crossed_terms(rows):
    middle = rows // 2
    upper = [
        (h, [(0, h + 1, 0)] + ([(1, h, 1)] if h < middle else [])) for h in range(rows - 1)
    ]
    lower = [
        (h, [(0, h - 1, 2)] + ([(1, h, 1)] if h >= middle else [])) for h in range(1, rows)
    ]
    return upper, lower


def crossed_steps(units, m, part, numbers, w_ref, slot, block, depth, rows, flat_row):
    khs = ((0, 1), (2, 1))[part]
    heights = [h for h, _ in crossed_terms(rows)[part]]
    for chunks in in_pairs(range(depth)):
        yield 0, lambda chunks=chunks: units.weights(
            m, crossed(w_ref, slot, block, khs, chunks))
        for h in heights:
            yield 1, lambda chunks=chunks, h=h: units.add(m, numbers[h], beside(
                [flat_row(h)[:, c * LANES : (c + 1) * LANES] for c in chunks]), h == heights[0])


def crossed_pops(units, places, rows, give):
    items = []
    for part, (m, numbers) in enumerate(places):
        for h, uses in crossed_terms(rows)[part]:
            items.append((m, numbers[h], uses))
    order = [r for _, _, uses in items for _, r, _ in uses]
    seen = 0
    for m, number, uses in items:
        product = units.pop(m, number)
        for half, r, kh in uses:
            term = product[:, half * LANES : (half + 1) * LANES]
            give(r, kh, term, r not in order[:seen], r not in order[seen + 1 :])
            seen += 1


def halo_jobs(frames, depth):
    run = lambda f, slots: [(f, chunk, slots) for chunk in range(depth)]
    wide = [
        (sum((run(f, (g - f, g - f)) for f in range(max(0, g + 1 - TAPS), g + 1)), []), (0, 1), (g, g))
        for g in range(frames)
    ]
    thin = [(run(f, (0, 1)), (2, 2), (f, f + 1)) for f in range(frames - 1)]
    alone = {}
    for f, slot in [(f, 2) for f in range(frames - 2)] + [(frames - 1, 0)]:
        alone[f + slot] = alone.get(f + slot, []) + run(f, (slot,))
    second = wide[:1] + thin
    for g, entries in alone.items():
        second.append((entries, (2,), (g,)))
    second.sort(key=lambda job: (max(f for f, _, _ in job[0]), len(job[1]) < 2))
    return wide[1:], second


def halo_steps(units, m, jobs, w_ref, kh, flat_ref, give):
    for number, (entries, blocks, made) in enumerate(jobs):
        number = number % ACCS
        for pair in in_pairs(entries):
            def operand(pair=pair, blocks=blocks):
                columns = []
                for j, block in enumerate(blocks):
                    parts = [
                        w_ref[TAPS - 1 - slots[j], kh, chunk * LANES : (chunk + 1) * LANES,
                              block * LANES : (block + 1) * LANES]
                        for _, chunk, slots in pair
                    ]
                    while len(parts) < 2:
                        parts.append(jnp.zeros((LANES, LANES), BF16))
                    columns.append(jnp.concatenate(parts, axis=0))
                while len(columns) < 2:
                    columns.append(jnp.zeros((SIDE, LANES), BF16))
                units.weights(m, jnp.concatenate(columns, axis=1))

            def multiply(pair=pair, number=number):
                units.add(m, number, beside([
                    flat_ref[f, :, chunk * LANES : (chunk + 1) * LANES] for f, chunk, _ in pair]), True)

            yield 0, operand
            yield 1, multiply

        def hand(number=number, blocks=blocks, made=made):
            product = units.pop(m, number)
            for j, (block, g) in enumerate(zip(blocks, made)):
                give(g, block, product[:, j * LANES : (j + 1) * LANES])

        yield 0, hand


def halo_shares(frames, depth):
    shares = {}
    for jobs in halo_jobs(frames, depth):
        for _, blocks, made in jobs:
            for key in zip(made, blocks):
                shares[key] = shares.get(key, 0) + 1
    return shares


def merged(streams, step):
    streams = [list(stream) for stream in streams]
    totals = [max(1, sum(cost for cost, _ in stream)) for stream in streams]
    spent = [0] * len(streams)
    while any(streams):
        live = [i for i, stream in enumerate(streams) if stream]
        i = min(live, key=lambda i: spent[i] / totals[i])
        cost, run = streams[i].pop(0)
        run()
        spent[i] += cost
        if cost:
            step()


def select(x_hbm, far_ref, near_ref, sem):
    frames, rows = x_hbm.shape[:2]
    odd = parity()
    copies = []
    for place, (target, row) in enumerate(
        ((far_ref, odd * (rows - 1)), (near_ref, (1 - odd) * (rows - 1)))
    ):
        copies.append(pltpu.make_async_copy(x_hbm.at[:, row], target, sem.at[place]))
        copies[-1].start()
    for copy in copies:
        copy.wait()


def interior(
    inter_ref, ramp_ref, x_ref, near_ref, w_ref, gamma_ref, bias_ref,
    out_hbm, part_ref, last_ref, carry_ref, nacc_ref, late_ref,
    line, flat, nflat, acc, done_s, o_sem,
):
    frames, rows, width, chans = x_ref.shape
    depth = TAPS * chans // LANES
    passes = conv_passes(depth)
    _, below_first, below_second, _ = scales(inter_ref, ramp_ref)
    below = (below_first, below_second)
    gamma = 0.5 * gamma_ref[...]
    clear_ends(line)
    near_kh = 2 * (1 - parity())

    def flat_at(f, h):
        return last_ref.at[h] if f == frames - 1 else flat.at[f, h]

    queue = Queue()
    ready = {}
    for f in range(frames):
        for h in reversed(range(rows)):
            ready[f, h] = queue.add(
                prepare(x_ref.at[f, h], gamma, line.at[h], flat_at(f, h)))
        ready[f] = queue.add(prepare(near_ref.at[f], gamma, line.at[rows], nflat.at[f]))

    def weight(tile, places):
        return cells(w_ref, tile, places)

    def contribute(g, r, lanes, term, first, final):
        total, at = (carry_ref, (r,)) if g == frames - 1 else (acc, (g, r))
        at = at + (slice(None), lanes)
        if first:
            term = term + (x_ref[g, r, :, lanes].astype(F32) + bias_ref[:, lanes])
        else:
            term = term + total[at]
        if not final:
            total[at] = term
        elif r == 0:
            part_ref[g, 0, :, lanes] = term
        elif r == rows - 1:
            part_ref[g, 1, :, lanes] = term
        elif g == frames - 2:
            late_ref[r - 1, :, lanes] = term.astype(BF16)
        else:
            done_s[g, r - 1, :, lanes] = term.astype(BF16)

    def run(*accs):
        units = Units(accs)

        def pop(f, m, tile, number, r, last):
            product = units.pop(m, number)
            for i, (slot, block) in enumerate(tile):
                lanes = slice(block * LANES, (block + 1) * LANES)
                term = product[:, i * LANES : (i + 1) * LANES]
                if number >= 4:
                    term = term * below[r]
                contribute(
                    f + slot, r, lanes, term,
                    (f == 0 or slot == 2) and number < 4, slot == 0 and last)

        queue.until(ready[0, 0])
        copies = []
        for f in range(frames - 1):
            jobs = jobs_of(tiles_of(chans, min(TAPS, frames - f)), rows)
            for place, job in enumerate(jobs):
                flat_row = lambda h: flat.at[f, h]
                if f:
                    queue.until(ready[f, 0])
                matrix_job(
                    units, job, passes, rows, flat_row, weight,
                    lambda: queue.some(RATE), lambda *rest: pop(f, *rest))
            tile = tiles_of(chans, min(TAPS, frames - f))[-1]
            if len(tile) == 1:
                (slot, block), = tile
                numbers = {h: h for h in range(rows)}
                flat_row = lambda h: flat.at[f, h]
                merged([
                    crossed_steps(
                        units, part, part, numbers, w_ref, slot, block, depth, rows, flat_row)
                    for part in range(MXUS)
                ], lambda: queue.some(RATE))

                def give(r, kh, term, first, last):
                    if kh == 2 and r < 2:
                        term = term * below[r]
                    contribute(
                        f + slot, r, slice(block * LANES, (block + 1) * LANES), term,
                        first and (f == 0 or slot == 2), last and slot == 0)

                crossed_pops(units, [(0, numbers), (1, numbers)], rows, give)
            if f < frames - 2:
                copies.append(pltpu.make_async_copy(
                    done_s.at[f], out_hbm.at[f, pl.ds(1, rows - 2)], o_sem.at[f]))
                copies[-1].start()
        queue.until(len(queue.items))
        seen = set()

        def near(g, block, term):
            lanes = slice(block * LANES, (block + 1) * LANES)
            if (g, block) in seen:
                term = term + nacc_ref[g, :, lanes]
            seen.add((g, block))
            nacc_ref[g, :, lanes] = term

        merged([
            halo_steps(units, m, jobs, w_ref, near_kh, nflat, near)
            for m, jobs in enumerate(halo_jobs(frames, depth))
        ], lambda: None)
        for copy in copies:
            copy.wait()

    pl.run_scoped(run, *[pltpu.ACC(m)((width, SIDE), F32) for m in range(MXUS) for _ in range(ACCS)])


def edges(
    inter_ref, ramp_ref, far_ref, w_ref, gamma_ref, part_ref, last_ref, carry_ref, nacc_ref, late_ref, _,
    out_hbm,
    line, fflat, acc, facc, tail, done_s, inner_s, o_sem, i_sem, l_sem,
):
    frames, width, chans = far_ref.shape
    rows = out_hbm.shape[1]
    depth = TAPS * chans // LANES
    passes = conv_passes(depth)
    odd = parity()
    top, below_first, below_second, bottom = scales(inter_ref, ramp_ref)
    below = (below_first, below_second)
    far_scale = jnp.where(odd == 1, bottom, top)
    near_scale = jnp.where(odd == 1, top, bottom)
    gamma = 0.5 * gamma_ref[...]
    clear_ends(line)
    final = frames - 1
    late = pltpu.make_async_copy(late_ref, out_hbm.at[final - 1, pl.ds(1, rows - 2)], l_sem)
    late.start()
    blocks = [slice(b * LANES, (b + 1) * LANES) for b in range(chans // LANES)]

    queue = Queue()
    ready = [
        queue.add(prepare(far_ref.at[f], gamma, line.at[0], fflat.at[f])) for f in range(frames)
    ]

    def near_row(g, at):
        span = slice(at, at + CHUNK)
        for lanes in blocks:
            base = tail[1 - odd, span, lanes] if g == final else part_ref[g, 1 - odd, span, lanes]
            total = base + near_scale * nacc_ref[g, span, lanes]
            done_s[g, 1 - odd, span, lanes] = total.astype(BF16)

    def run(*accs):
        units = Units(accs)

        def contribute(r, lanes, term, first, last):
            term = term + (carry_ref if first else acc)[r, :, lanes]
            if not last:
                acc[r, :, lanes] = term
            elif r == 0 or r == rows - 1:
                tail[0 if r == 0 else 1, :, lanes] = term
            else:
                inner_s[r - 1, :, lanes] = term.astype(BF16)
            if last:
                made.append(r)
                if len(made) == rows * len(blocks):
                    settle()

        def pop(m, tile, number, r, kept, last):
            product = units.pop(m, number)
            for i, (_, block) in enumerate(tile):
                term = product[:, i * LANES : (i + 1) * LANES]
                contribute(r, blocks[block], term * below[r] if kept else term, not kept, last)

        def taps(m, tile, rows_of, numbers):
            for number, places in enumerate(passes):
                active = [r for r in rows_of if acc_of(r, places, rows) is not None]
                if active:
                    yield 0, lambda places=places: units.weights(m, cells(w_ref, tile, places))
                for r in active:
                    yield 1, lambda r=r, places=places, active=active: units.add(
                        m, numbers[acc_of(r, places, rows)], row_block(flat_row, r, places), r == active[0])
                for r in active:
                    here = acc_of(r, places, rows)
                    later = [acc_of(r, other, rows) for other in passes[number + 1 :]]
                    if here not in later:
                        yield 0, lambda r=r, here=here, last=all(o is None for o in later): pop(
                            m, tile, numbers[here], r, here >= rows, last)

        flat_row = lambda h: last_ref.at[h]
        first_tile, rest = tiles_of(chans, 1)
        (_, block), = rest
        upper = {h: h for h in range(rows)}
        lower = {h: 2 + h for h in range(rows)}

        def give(r, kh, term, first, last):
            contribute(r, blocks[block], term * below[r] if kh == 2 and r < 2 else term, first, last)

        def second():
            for part, numbers in enumerate((upper, lower)):
                yield from crossed_steps(
                    units, 1, part, numbers, w_ref, 0, block, depth, rows, flat_row)
            yield 0, lambda: crossed_pops(units, [(1, upper), (1, lower)], rows, give)
            yield from taps(1, first_tile, [0], {0: 0, 4: 1})

        copies, made = [], []
        inner = pltpu.make_async_copy(
            inner_s, out_hbm.at[final, pl.ds(1, rows - 2)], i_sem)

        def send(g, kind):
            side = (1 - odd, odd)[kind]
            copies.append(pltpu.make_async_copy(
                done_s.at[g, side], out_hbm.at[g, side * (rows - 1)], o_sem.at[g, kind]))
            copies[-1].start()

        def settle():
            inner.start()
            for g in range(frames):
                queue.add([lambda g=g, at=at: near_row(g, at) for at in range(0, width, CHUNK)])
                queue.add([lambda g=g: send(g, 0)])

        shares = halo_shares(frames, depth)
        seen = {}

        def collect(g, block, term):
            lanes = blocks[block]
            seen[g, block] = seen.get((g, block), 0) + 1
            if seen[g, block] > 1:
                term = term + facc[g, :, lanes]
            if seen[g, block] < shares[g, block]:
                facc[g, :, lanes] = term
                return
            base = tail[odd, :, lanes] if g == final else part_ref[g, odd, :, lanes]
            done_s[g, odd, :, lanes] = (base + far_scale * term).astype(BF16)
            if all(seen.get((g, b)) == shares[g, b] for b in range(len(blocks))):
                send(g, 1)

        def halo(m):
            yield 0, lambda: queue.until(ready[-1])
            yield from halo_steps(
                units, m, halo_jobs(frames, depth)[m], w_ref, 2 * odd, fflat, collect)

        merged([
            itertools.chain(taps(0, first_tile, [3, 1, 2], {r: r for r in range(ACCS)}), halo(0)),
            itertools.chain(second(), halo(1)),
        ], lambda: queue.some(RATE))
        queue.until(len(queue.items))
        inner.wait()
        for copy in copies:
            copy.wait()
        late.wait()

    pl.run_scoped(run, *[pltpu.ACC(m)((width, SIDE), F32) for m in range(MXUS) for _ in range(ACCS)])


def per_device(latents, gamma, weight, bias, intersection, ramp):
    frames, rows, width, chans = latents.shape
    deep = TAPS * chans
    gamma = gamma.reshape(1, chans)
    bias = bias.reshape(1, chans)
    weight = weight.reshape(TAPS, TAPS, deep, chans)
    count = lax.axis_size("rows")
    smem = pl.BlockSpec(memory_space=pltpu.SMEM)
    vmem = pl.BlockSpec(memory_space=pltpu.VMEM)
    hbm = pl.BlockSpec(memory_space=pltpu.HBM)
    anywhere = pl.BlockSpec(memory_space=pl.ANY)
    dma = pltpu.SemaphoreType.DMA
    inside = lambda array: pltpu.with_memory_space_constraint(array, pltpu.VMEM)
    outside = lambda array: pltpu.with_memory_space_constraint(array, pltpu.HBM)
    swap = lambda array, start: lax.ppermute(array, "rows", [
        pair for k in range(start, count - 1, 2) for pair in ((k, k + 1), (k + 1, k))])
    halo = pltpu.VMEM((frames, width, chans), BF16)
    far, near = pl.pallas_call(
        select,
        out_shape=(halo, halo),
        in_specs=[hbm],
        out_specs=(vmem, vmem),
        scratch_shapes=[dma((2,))],
        cost_estimate=pl.CostEstimate(flops=20 * 10**9, bytes_accessed=4 * 2**20, transcendentals=0),
        compiler_params=pltpu.CompilerParams(vmem_limit_bytes=2**20),
        name="select",
    )(outside(latents))
    weight = inside(weight)
    near = swap(near, 0)
    far = swap(far, 1)
    out, part, last, carry, nacc, late = pl.pallas_call(
        interior,
        out_shape=(
            jax.ShapeDtypeStruct(latents.shape, BF16),
            pltpu.VMEM((frames - 1, 2, width, chans), F32),
            pltpu.VMEM((rows, width, deep), BF16),
            pltpu.VMEM((rows, width, chans), F32),
            pltpu.VMEM((frames, width, chans), F32),
            pltpu.VMEM((rows - 2, width, chans), BF16),
        ),
        in_specs=[smem, smem, vmem, vmem, vmem, vmem, vmem],
        out_specs=(anywhere,) + (vmem,) * 5,
        scratch_shapes=[
            pltpu.VMEM((rows + 1, chans // LANES, width + 16, LANES), F32),
            pltpu.VMEM((frames - 1, rows, width, deep), BF16),
            pltpu.VMEM((frames, width, deep), BF16),
            pltpu.VMEM((frames - 1, rows, width, chans), F32),
            pltpu.VMEM((frames - 2, rows - 2, width, chans), BF16),
            dma((frames - 2,)),
        ],
        cost_estimate=pl.CostEstimate(
            flops=2 * 84 * width * deep * chans, bytes_accessed=14 * 2**20, transcendentals=0
        ),
        compiler_params=pltpu.CompilerParams(vmem_limit_bytes=24 * 2**20),
        name="interior",
    )(intersection, ramp, inside(latents), inside(near), weight, gamma, bias)
    return pl.pallas_call(
        edges,
        out_shape=jax.ShapeDtypeStruct(latents.shape, BF16),
        in_specs=[smem, smem] + [vmem] * 8 + [anywhere],
        out_specs=anywhere,
        input_output_aliases={10: 0},
        scratch_shapes=[
            pltpu.VMEM((1, chans // LANES, width + 16, LANES), F32),
            pltpu.VMEM((frames, width, deep), BF16),
            pltpu.VMEM((rows, width, chans), F32),
            pltpu.VMEM((frames, width, chans), F32),
            pltpu.VMEM((2, width, chans), F32),
            pltpu.VMEM((frames, 2, width, chans), BF16),
            pltpu.VMEM((rows - 2, width, chans), BF16),
            dma((frames, 2)),
            dma(()),
            dma(()),
        ],
        cost_estimate=pl.CostEstimate(
            flops=2 * 24 * width * deep * chans, bytes_accessed=4 * 2**20, transcendentals=0
        ),
        compiler_params=pltpu.CompilerParams(vmem_limit_bytes=16 * 2**20),
        name="edges",
    )(
        intersection, ramp, inside(far), weight, gamma, inside(part), inside(last),
        inside(carry), inside(nacc), inside(late), out,
    )


def solution(mesh):
    in_specs = (P("clips", "rows", None, None), P(), P(), P(), P("clips"), P("clips"))
    out_specs = P("clips", "rows", None, None)
    return jax.shard_map(
        per_device, mesh=mesh, in_specs=in_specs, out_specs=out_specs, check_vma=False
    )
```
